512 devices in a mesh: dp: 32 (over z_hi, x, core), code: 16 (over z_lo, y).
Axes of the slice: x: 4, y: 8, z: 8 (z_hi: 4, z_lo: 2; z = z_hi * 2 + z_lo), core: 2. Of those that a mesh axis runs over, the one named last changes fastest.
Arguments:
- latents: bfloat16 [16384, 128], P(('dp', 'code')), may hold values from -240 to 240
- basis: bfloat16 [131072, 128], P('code'), may hold values from -6 to 6
- code_map: bfloat16 [128, 128], replicated, may hold values from -0.5 to 0.5
Outputs:
- quantized: bfloat16 [16384, 128], P(('dp', 'code'))
- usage: float32 [131072], P('code')
- map_grad: float32 [4096, 128], P('dp')
The draws below stay inside these ranges and needn't reach their ends.
All inputs are finite; a program needn't handle non-finite values.
Results may differ from the reference program's by a relative error of at most 0.023.
The reference program's roundings to bfloat16 on the way count: a program that leaves them out, or rounds other values in their place, can miss the bound.
Values may be sent and summed in bfloat16 or wider, within the bound.
A program may use at most 64 MiB of HBM per device.

```python
import jax
import jax.numpy as jnp
from jax import lax

D = 128
TOK_DP = 512
CODES = 131072
TOKENS = 16384
GRAD_ROWS = 4096


def draw_latents(key, part):
    key = jax.random.fold_in(key, 11)
    first = jax.random.fold_in(key, 0)
    values = jnp.clip(jax.random.normal(first, (TOKENS, D), jnp.float32), -6.0, 6.0)
    return values.astype(jnp.bfloat16)


def shard_levels(rng, extent, shards, low, high):
    gain = 1.0
    for position, blocks in shards:
        draws = jax.random.uniform(jax.random.fold_in(jax.random.fold_in(rng, 6), position), (blocks,), jnp.float32, low / len(shards), high / len(shards))
        gain = gain * jnp.repeat(jnp.exp(draws), extent[position] // blocks).reshape((-1,) + (1,) * (len(extent) - 1 - position))
    return gain


def scatter_about(stream_key, dims, scale, reach, cuts=(), kind=jnp.bfloat16):
    entries = jax.random.normal(stream_key, dims, jnp.float32) * scale
    if len(cuts) > 0:
        entries = shard_levels(stream_key, dims, cuts, -0.22, 0.18) * entries
    return jnp.clip(entries, min=-reach, max=reach).astype(kind)


def setup_inputs(seed: int = 0) -> dict:
    keys = jax.random.split(jax.random.key(seed), 4)
    latents = draw_latents(jax.random.fold_in(keys[3], 71), 0)
    basis = scatter_about(keys[1], (CODES, D), 1.0, 6.0, ((0, 16),))
    code_map = scatter_about(keys[2], (D, D), D ** -0.5, 0.5)
    return dict(latents=latents, basis=basis, code_map=code_map)


def reference(latents, basis, code_map):
    codebook = jnp.dot(basis, code_map, preferred_element_type=jnp.float32).astype(jnp.bfloat16)
    code_f = codebook.astype(jnp.float32)
    code_sq = lax.optimization_barrier(jnp.sum(code_f * code_f, axis=1))
    basis_f = basis.astype(jnp.float32)
    tiles = latents.reshape(TOKENS // TOK_DP, TOK_DP, D)

    def one_tile(usage_acc, tile):
        dots = lax.dot_general(tile, codebook, (((1,), (1,)), ((), ())), preferred_element_type=jnp.float32)
        scores = (2.0 * dots - code_sq[None, :]) / 16.0
        row_top = lax.optimization_barrier(jnp.max(scores, axis=1, keepdims=True))
        weights = jnp.exp(scores - row_top)
        row_total = lax.optimization_barrier(jnp.sum(weights, axis=1, keepdims=True))
        assign = weights / row_total
        soft = jnp.dot(assign, code_f, precision=lax.Precision.HIGHEST)
        errors = (soft - tile.astype(jnp.float32)).astype(jnp.bfloat16)
        code_err = lax.dot_general(assign.astype(jnp.bfloat16), errors, (((0,), (0,)), ((), ())), preferred_element_type=jnp.float32)
        tile_grad = lax.dot_general(basis_f, code_err, (((0,), (0,)), ((), ())), precision=lax.Precision.HIGHEST) / jnp.sqrt(jnp.float32(TOK_DP))
        return (usage_acc + lax.optimization_barrier(jnp.sum(assign, axis=0)), (soft.astype(jnp.bfloat16), tile_grad))
    usage_sum, (quant, grads) = lax.scan(one_tile, jnp.zeros((CODES,), jnp.float32), tiles)
    usage = usage_sum * (CODES / TOKENS)
    return (quant.reshape(TOKENS, D), usage, grads.reshape(GRAD_ROWS, D))
```

```python
import functools
import math

import jax
import jax.numpy as jnp
from jax import lax
from jax.experimental import pallas as pl
from jax.experimental.pallas import tpu as pltpu
from jax.sharding import PartitionSpec as P

MESH = pl.DeviceIdType.MESH
F32 = jnp.float32
BF16 = jnp.bfloat16
NT = (((1,), (1,)), ((), ()))
TN = (((0,), (0,)), ((), ()))
LANES = 128
KB = 1024
LOG2E = math.log2(math.e)


def dot(a, b, dims=(((1,), (0,)), ((), ()))):
    return lax.dot_general(a, b, dims, preferred_element_type=F32)


def split_three(values):
    upper = values.astype(BF16)
    rest = values - upper.astype(F32)
    middle = rest.astype(BF16)
    lower = (rest - middle.astype(F32)).astype(BF16)
    return (upper, middle, lower)


def wide(column, width):
    return jnp.concatenate([column] * (width // LANES), axis=1)


def wait_bytes(ref, sem):
    pltpu.make_async_copy(ref, ref, sem).wait()


def make_codebook(i, bext, cmap, cb, sq):
    code = dot(bext[i, :, :LANES], cmap[...]).astype(BF16)
    cb[i] = code
    wide_code = code.astype(F32)
    square = wide_code * wide_code
    upper = square.astype(BF16)
    lower = (square - upper.astype(F32)).astype(BF16)
    ones = jnp.full((16, 2 * LANES), -0.0625, BF16)
    total = dot(ones, jnp.concatenate([upper, lower], axis=1), NT)
    sq[i] = total[:8]


def score_block(i, x8, cb, sq, s_buf, top):
    s = dot(x8[...], cb[i], NT) + sq[i, 0:1, :]
    s_buf[i] = s
    best = s[:, :LANES]
    for j in range(1, KB // LANES):
        best = jnp.maximum(best, s[:, j * LANES:(j + 1) * LANES])
    top[...] = jnp.maximum(top[...], best)


def weight_block(i, s_buf, top, w_buf, bext, acc):
    w = jnp.exp(s_buf[i] - wide(top[...], KB)).astype(BF16)
    w_buf[i] = w
    acc[...] += dot(w, bext[i])


def lanes_of(columns):
    rows = columns.shape[0]
    eye = lax.broadcasted_iota(jnp.int32, (LANES, LANES), 0) == lax.broadcasted_iota(
        jnp.int32, (LANES, LANES), 1
    )
    out = []
    for g in range(rows // LANES):
        part = jnp.where(eye, columns[g * LANES:(g + 1) * LANES], 0.0)
        out.append(jnp.sum(part, axis=0, keepdims=True))
    return jnp.concatenate(out, axis=0)


def usage_block(i, r3, w_buf, u_part):
    u = jnp.sum(dot(r3, w_buf[i]), axis=0, keepdims=True)
    width = u_part.shape[2]
    per = KB // width
    for j in range(per):
        u_part[i * per + j] = u[:, j * width:(j + 1) * width]


def kernel(n_dp, n_code, x_ref, basis_ref, map_ref, q_ref, u_ref, g_ref,
           bext, cmap, cb, sq, x_all, x8, s_buf, top, w_buf, acc,
           lse, w_send, w_recv, fac, w_all, q_buf, g_buf, u_part, u_recv, u_all,
           load_sem, out_sem, send_sem, recv_sem):
    dp = lax.axis_index("dp")
    code = lax.axis_index("code")
    nblk = basis_ref.shape[0] // KB
    rows = x_ref.shape[0]
    tokens = rows * n_code

    x_load = pltpu.make_async_copy(x_ref, x_all.at[code], load_sem.at[nblk])
    m_load = pltpu.make_async_copy(map_ref, cmap, load_sem.at[nblk + 1])
    x_load.start()
    m_load.start()

    def basis_load(i):
        return pltpu.make_async_copy(
            basis_ref.at[pl.ds(i * KB, KB)], bext.at[i, :, pl.ds(0, LANES)], load_sem.at[i]
        )

    for i in range(nblk):
        basis_load(i).start()

    barrier = pltpu.get_barrier_semaphore()

    def greet_code(i, _):
        peer = lax.rem(code + i, n_code)
        pl.semaphore_signal(barrier, inc=1, device_id=(dp, peer), device_id_type=MESH)
        return 0

    def greet_dp(i, _):
        peer = lax.rem(dp + i, n_dp)
        pl.semaphore_signal(barrier, inc=1, device_id=(peer, code), device_id_type=MESH)
        return 0

    lax.fori_loop(1, n_code, greet_code, 0)
    lax.fori_loop(1, n_dp, greet_dp, 0)

    for i in range(nblk):
        bext[i, :, LANES:] = jnp.ones((KB, LANES), BF16)
    x_load.wait()
    m_load.wait()
    pl.semaphore_wait(barrier, n_code + n_dp - 2)

    def to_code(phase, src, dst):
        def send(i, _):
            peer = lax.rem(code + i, n_code)
            pltpu.make_async_remote_copy(
                src_ref=src(peer), dst_ref=dst, send_sem=send_sem.at[phase],
                recv_sem=recv_sem.at[phase], device_id=(dp, peer), device_id_type=MESH,
            ).start()
            return 0
        lax.fori_loop(1, n_code, send, 0)

    def to_dp(phase, src, dst):
        def send(i, _):
            peer = lax.rem(dp + i, n_dp)
            pltpu.make_async_remote_copy(
                src_ref=src(peer), dst_ref=dst, send_sem=send_sem.at[phase],
                recv_sem=recv_sem.at[phase], device_id=(peer, code), device_id_type=MESH,
            ).start()
            return 0
        lax.fori_loop(1, n_dp, send, 0)

    others_code = pl.ds(0, n_code - 1)
    others_dp = pl.ds(0, n_dp - 1)

    to_code(0, lambda peer: x_all.at[code], x_all.at[code])

    def codebook_step(i, _):
        basis_load(i).wait()
        make_codebook(i, bext, cmap, cb, sq)
        return 0

    lax.fori_loop(0, nblk, codebook_step, 0)
    top[...] = jnp.full_like(top, -jnp.inf)
    acc[...] = jnp.zeros_like(acc)

    wait_bytes(x_all.at[others_code], recv_sem.at[0])
    x8[...] = x_all[...].reshape(tokens, LANES) * jnp.asarray(0.125, BF16)

    def score_step(i, _):
        score_block(i, x8, cb, sq, s_buf, top)
        return 0

    lax.fori_loop(0, nblk, score_step, 0)
    top[...] = jnp.broadcast_to(jnp.max(top[...], axis=1, keepdims=True), top.shape)

    def weight_step(i, _):
        weight_block(i, s_buf, top, w_buf, bext, acc)
        return 0

    lax.fori_loop(0, nblk, weight_step, 0)

    groups = tokens // LANES
    lse[code] = jnp.concatenate([lanes_of(top[...]), lanes_of(acc[:, LANES:])], axis=0)
    to_code(1, lambda peer: lse.at[code], lse.at[code])
    w_send[...] = acc[:, :LANES].astype(BF16).reshape(n_code, rows, LANES)
    to_code(2, lambda peer: w_send.at[peer], w_recv.at[code])
    w_recv[code] = w_send[code]

    wait_bytes(lse.at[others_code], recv_sem.at[1])
    tops = lse[:, :groups, :]
    best = jnp.max(tops, axis=0)
    factor = jnp.exp(tops - best[None])
    total = jnp.sum(factor * lse[:, groups:, :], axis=0)
    own = jnp.exp(lse[code, :groups, :] - best) / total
    own_row = jnp.concatenate([own[g:g + 1] for g in range(groups)], axis=1)
    place = lax.broadcasted_iota(jnp.int32, (16, tokens), 0)
    r3 = jnp.zeros((16, tokens), F32)
    for j, piece in enumerate(split_three(own_row)):
        r3 = jnp.where(place == j, jnp.broadcast_to(piece.astype(F32), r3.shape), r3)
    r3 = r3.astype(BF16)

    def usage_step(i, _):
        usage_block(i, r3, w_buf, u_part)
        return 0

    lax.fori_loop(0, nblk, usage_step, 0)
    to_dp(3, lambda peer: u_part.at[peer], u_recv.at[dp])
    u_recv[dp] = u_part[dp]

    scaled = factor / total[None]
    for g in range(groups):
        fac[g, :n_code] = scaled[:, g, :]
        fac[g, n_code:] = jnp.zeros((LANES - n_code, LANES), F32)
    per = LANES // rows
    turned = jnp.transpose(fac[code // per])
    fac[0] = turned
    mine = fac[0, pl.ds(pl.multiple_of(lax.rem(code, per) * rows, rows), rows), :]

    wait_bytes(w_recv.at[others_code], recv_sem.at[2])
    w_own = jnp.zeros((rows, LANES), F32)
    for c in range(n_code):
        w_own = w_own + mine[:, c:c + 1] * w_recv[c].astype(F32)
    w_all[code] = w_own.astype(BF16)
    to_code(4, lambda peer: w_all.at[code], w_all.at[code])

    soft_own = jnp.zeros((rows, LANES), F32)
    for piece in split_three(w_own):
        soft_own = soft_own + dot(piece, cmap[...])
    q_buf[...] = soft_own.astype(BF16)
    q_out = pltpu.make_async_copy(q_buf, q_ref, out_sem.at[0])
    q_out.start()

    wait_bytes(u_recv.at[others_dp], recv_sem.at[3])
    scale = (basis_ref.shape[0] * n_code) / (tokens * n_dp)
    u_all[dp] = jnp.sum(u_recv[...], axis=0) * scale
    to_dp(5, lambda peer: u_all.at[dp], u_all.at[dp])

    wait_bytes(w_all.at[others_code], recv_sem.at[4])
    w_tile = w_all[...].reshape(tokens, LANES)
    x_tile = x_all[...].reshape(tokens, LANES)
    errors = (dot(w_tile, cmap[...]) - x_tile.astype(F32)).astype(BF16)
    g_buf[...] = dot(w_tile, errors, TN) * (1.0 / math.sqrt(tokens))
    g_out = pltpu.make_async_copy(g_buf, g_ref, out_sem.at[1])
    g_out.start()

    wait_bytes(u_all.at[others_dp], recv_sem.at[5])
    u_out = pltpu.make_async_copy(u_all, u_ref, out_sem.at[2])
    u_out.start()

    wait_bytes(x_all.at[others_code], send_sem.at[0])
    wait_bytes(lse.at[others_code], send_sem.at[1])
    wait_bytes(w_send.at[others_code], send_sem.at[2])
    wait_bytes(u_part.at[others_dp], send_sem.at[3])
    wait_bytes(w_all.at[others_code], send_sem.at[4])
    wait_bytes(u_all.at[others_dp], send_sem.at[5])
    q_out.wait()
    g_out.wait()
    u_out.wait()


def body(n_dp, n_code, latents, basis, code_map):
    rows, width = latents.shape
    kdev = basis.shape[0]
    nblk = kdev // KB
    tokens = rows * n_code
    chunk = kdev // n_dp
    vm = pltpu.VMEM
    quantized, usage, grad = pl.pallas_call(
        functools.partial(kernel, n_dp, n_code),
        out_shape=(
            jax.ShapeDtypeStruct((rows, width), BF16),
            jax.ShapeDtypeStruct((n_dp, 1, chunk), F32),
            jax.ShapeDtypeStruct((width, width), F32),
        ),
        in_specs=[pl.BlockSpec(memory_space=pl.ANY)] * 3,
        out_specs=[pl.BlockSpec(memory_space=pl.ANY)] * 3,
        scratch_shapes=[
            vm((nblk, KB, 2 * width), BF16),
            vm((width, width), BF16),
            vm((nblk, KB, width), BF16),
            vm((nblk, 8, KB), F32),
            vm((n_code, rows, width), BF16),
            vm((tokens, width), BF16),
            vm((nblk, tokens, KB), F32),
            vm((tokens, LANES), F32),
            vm((nblk, tokens, KB), BF16),
            vm((tokens, 2 * width), F32),
            vm((n_code, 2 * tokens // LANES, LANES), F32),
            vm((n_code, rows, width), BF16),
            vm((n_code, rows, width), BF16),
            vm((tokens // LANES, LANES, LANES), F32),
            vm((n_code, rows, width), BF16),
            vm((rows, width), BF16),
            vm((width, width), F32),
            vm((n_dp, 1, chunk), F32),
            vm((n_dp, 1, chunk), F32),
            vm((n_dp, 1, chunk), F32),
            pltpu.SemaphoreType.DMA((nblk + 2,)),
            pltpu.SemaphoreType.DMA((3,)),
            pltpu.SemaphoreType.DMA((6,)),
            pltpu.SemaphoreType.DMA((6,)),
        ],
        compiler_params=pltpu.CompilerParams(
            collective_id=0, has_side_effects=True, vmem_limit_bytes=56 * 1024 * 1024
        ),
    )(latents, basis, code_map)
    return (quantized, usage.reshape(kdev), grad)


def solution(mesh):
    return jax.shard_map(
        functools.partial(body, mesh.shape["dp"], mesh.shape["code"]),
        mesh=mesh,
        in_specs=(P(("dp", "code"), None), P("code", None), P()),
        out_specs=(P(("dp", "code"), None), P("code"), P("dp", None)),
        check_vma=False,
    )
```

```python
import functools
import math

import jax
import jax.numpy as jnp
from jax import lax
from jax.experimental import pallas as pl
from jax.experimental.pallas import tpu as pltpu
from jax.sharding import PartitionSpec as P

MESH = pl.DeviceIdType.MESH
F32 = jnp.float32
BF16 = jnp.bfloat16
NN = (((1,), (0,)), ((), ()))
NT = (((1,), (1,)), ((), ()))
TN = (((0,), (0,)), ((), ()))
LANES = 128
CHUNK = 1024

RING = 8
NEAR = (
    ((0, 0), (0, 1), (0, 7), (1, 0)),
    ((0, 2), (0, 6), (1, 1), (1, 7)),
    ((0, 3), (0, 5), (1, 2), (1, 6)),
    ((0, 4), (1, 3), (1, 5), (1, 4)),
)
X = 4
ZH = 4


def dot(a, b, dims=NN):
    return lax.dot_general(a, b, dims, preferred_element_type=F32)


def split_three(values):
    upper = values.astype(BF16)
    rest = values - upper.astype(F32)
    middle = rest.astype(BF16)
    lower = (rest - middle.astype(F32)).astype(BF16)
    return (upper, middle, lower)


def wide(column, width):
    return jnp.concatenate([column] * (width // LANES), axis=1)


def wait_bytes(ref, sem):
    pltpu.make_async_copy(ref, ref, sem).wait()


def make_codebook(i, bas, cmap, cb, sq):
    part = slice(i * CHUNK, (i + 1) * CHUNK)
    code = dot(bas[part, :], cmap[...]).astype(BF16)
    cb[part, :] = code
    wide_code = code.astype(F32)
    square = wide_code * wide_code
    upper = square.astype(BF16)
    lower = (square - upper.astype(F32)).astype(BF16)
    ones = jnp.full((16, 2 * LANES), -0.0625, BF16)
    total = dot(ones, jnp.concatenate([upper, lower], axis=1), NT)
    sq[:, part] = total[:8]


def group_scores(x_group, cb, sq, s_buf):
    codes = cb.shape[0]
    s = dot(x_group, cb[...], NT) + sq[0:1, :]
    s_buf[...] = s
    best = s[:, :LANES]
    for j in range(1, codes // LANES):
        best = jnp.maximum(best, s[:, j * LANES:(j + 1) * LANES])
    return jnp.broadcast_to(jnp.max(best, axis=1, keepdims=True), best.shape)


def group_weights(top, s_buf, bas, w_buf, places, rows):
    codes = bas.shape[0]
    w = jnp.exp(s_buf[...] - wide(top, codes)).astype(BF16)
    for j, place in enumerate(places):
        w_buf[pl.ds(place, rows), :] = w[j * rows:(j + 1) * rows]
    return dot(w, jnp.concatenate([bas[...], jnp.ones((codes, LANES), BF16)], axis=1))


def lanes_of(columns):
    rows = columns.shape[0]
    eye = lax.broadcasted_iota(jnp.int32, (LANES, LANES), 0) == lax.broadcasted_iota(
        jnp.int32, (LANES, LANES), 1
    )
    out = []
    for g in range(rows // LANES):
        part = jnp.where(eye, columns[g * LANES:(g + 1) * LANES], 0.0)
        out.append(jnp.sum(part, axis=0, keepdims=True))
    return jnp.concatenate(out, axis=0)


def usage_half(r3, w_buf, start, out):
    width = w_buf.shape[1] // 2
    u = jnp.sum(dot(r3, w_buf[:, pl.ds(start, width)]), axis=0, keepdims=True)
    for j in range(width // LANES):
        out[j:j + 1, :] = u[:, j * LANES:(j + 1) * LANES]


def kernel(n_dp, n_code, x_ref, basis_ref, map_ref, q_ref, u_ref, g_ref,
           bas, cmap, cb, sq, x_all, s_buf, w_buf, m_col, t_col,
           lse, w_send, w_recv, fac, w_all, q_buf, g_buf,
           u_send, u_mine, u_pair, u_all, u_out,
           load_sem, out_sem, send_sem, recv_sem):
    dp = lax.axis_index("dp")
    code = lax.axis_index("code")
    z_lo, y = code // RING, lax.rem(code, RING)
    core = lax.rem(dp, 2)
    x_pos = lax.rem(dp // 2, X)
    z_hi = dp // (2 * X)
    spot = dp // 2
    codes = basis_ref.shape[0]
    nblk = codes // CHUNK
    rows = x_ref.shape[0]
    tokens = rows * n_code
    groups = tokens // LANES

    def peer_code(offset):
        return lax.rem(z_lo + offset[0], n_code // RING) * RING + lax.rem(y + offset[1], RING)

    owners = [[peer_code(o) for o in group] for group in NEAR]
    far_first = [p for group in reversed(owners) for p in reversed(group)][:-1]
    sibling = dp + 1 - 2 * core
    spots = [
        (lax.rem(z_hi + a, ZH) * X + lax.rem(x_pos + b, X)) * 2 + core
        for a in (2, 1, 3, 0) for b in (2, 1, 3, 0)
    ][:-1]

    x_load = pltpu.make_async_copy(x_ref, x_all.at[code], load_sem.at[nblk])
    m_load = pltpu.make_async_copy(map_ref, cmap, load_sem.at[nblk + 1])
    b_loads = [
        pltpu.make_async_copy(
            basis_ref.at[pl.ds(i * CHUNK, CHUNK)], bas.at[pl.ds(i * CHUNK, CHUNK)], load_sem.at[i]
        )
        for i in range(nblk)
    ]
    x_load.start()
    m_load.start()
    for load in b_loads:
        load.start()

    barrier = pltpu.get_barrier_semaphore()
    for p in far_first:
        pl.semaphore_signal(barrier, inc=1, device_id=(dp, p), device_id_type=MESH)
    for d in spots + [sibling]:
        pl.semaphore_signal(barrier, inc=1, device_id=(d, code), device_id_type=MESH)

    def remote(src, dst, phase, device):
        return pltpu.make_async_remote_copy(
            src_ref=src, dst_ref=dst, send_sem=send_sem.at[phase], recv_sem=recv_sem.at[phase],
            device_id=device, device_id_type=MESH,
        )

    x_load.wait()
    m_load.wait()
    pl.semaphore_wait(barrier, len(far_first) + len(spots) + 1)

    for g in reversed(range(len(NEAR))):
        for p, offset in zip(owners[g], NEAR[g]):
            if offset != (0, 0):
                remote(x_all.at[code], x_all.at[code], g, (dp, p)).start()

    for i in range(nblk):
        b_loads[i].wait()
        make_codebook(i, bas, cmap, cb, sq)

    for g, group in enumerate(owners):
        arriving = len(group) - (1 if g == 0 else 0)
        wait_bytes(x_all.at[pl.ds(0, arriving)], recv_sem.at[g])
        x_group = jnp.concatenate([x_all[o] for o in group], axis=0) * jnp.asarray(0.125, BF16)
        top = group_scores(x_group, cb, sq, s_buf)
        places = [pl.multiple_of(o * rows, rows) for o in group]
        acc = group_weights(top, s_buf, bas, w_buf, places, rows)
        sums = acc[:, :LANES].astype(BF16)
        for j, o in enumerate(group):
            part = slice(j * rows, (j + 1) * rows)
            m_col[pl.ds(places[j], rows), :] = top[part]
            t_col[pl.ds(places[j], rows), :] = acc[part, LANES:]
            w_send[o] = sums[part]

    lse[code] = jnp.concatenate([lanes_of(m_col[...]), lanes_of(t_col[...])], axis=0)
    for p in far_first:
        remote(lse.at[code], lse.at[code], 4, (dp, p)).start()
    for p in far_first:
        remote(w_send.at[p], w_recv.at[code], 5, (dp, p)).start()
    w_recv[code] = w_send[code]

    others = pl.ds(0, n_code - 1)
    wait_bytes(lse.at[others], recv_sem.at[4])
    tops = lse[:, :groups, :]
    best = jnp.max(tops, axis=0)
    factor = jnp.exp(tops - best[None])
    total = jnp.sum(factor * lse[:, groups:, :], axis=0)
    own = jnp.exp(lse[code, :groups, :] - best) / total
    own_row = jnp.concatenate([own[g:g + 1] for g in range(groups)], axis=1)
    place = lax.broadcasted_iota(jnp.int32, (16, tokens), 0)
    r3 = jnp.zeros((16, tokens), F32)
    for j, piece in enumerate(split_three(own_row)):
        r3 = jnp.where(place == j, jnp.broadcast_to(piece.astype(F32), r3.shape), r3)
    r3 = r3.astype(BF16)

    half = codes // 2
    usage_half(r3, w_buf, pl.multiple_of((1 - core) * half, half), u_send)
    pair = remote(u_send, u_pair, 6, (sibling, code))
    pair.start()
    usage_half(r3, w_buf, pl.multiple_of(core * half, half), u_mine)
    pair.wait_recv()
    u_all[spot] = (u_mine[...] + u_pair[...]).astype(BF16)
    for d in spots:
        remote(u_all.at[spot], u_all.at[spot], 7, (d, code)).start()

    scaled = factor / total[None]
    for g in range(groups):
        fac[g, :n_code] = scaled[:, g, :]
        fac[g, n_code:] = jnp.zeros((LANES - n_code, LANES), F32)
    per = LANES // rows
    fac[0] = jnp.transpose(fac[code // per])
    mine = fac[0, pl.ds(pl.multiple_of(lax.rem(code, per) * rows, rows), rows), :]

    wait_bytes(w_recv.at[others], recv_sem.at[5])
    w_own = jnp.zeros((rows, LANES), F32)
    for c in range(n_code):
        w_own = w_own + mine[:, c:c + 1] * w_recv[c].astype(F32)
    w_all[code] = w_own.astype(BF16)
    for p in far_first:
        remote(w_all.at[code], w_all.at[code], 8, (dp, p)).start()

    soft_own = jnp.zeros((rows, LANES), F32)
    for piece in split_three(w_own):
        soft_own = soft_own + dot(piece, cmap[...])
    q_buf[...] = soft_own.astype(BF16)
    q_out = pltpu.make_async_copy(q_buf, q_ref, out_sem.at[0])
    q_out.start()

    wait_bytes(u_all.at[pl.ds(0, len(spots))], recv_sem.at[7])
    scale = (codes * n_code) / (tokens * n_dp)
    u_out[...] = jnp.sum(u_all[...].astype(F32), axis=0) * scale
    u_copy = pltpu.make_async_copy(u_out, u_ref.at[core], out_sem.at[2])
    u_copy.start()
    u_far = remote(u_out, u_ref.at[core], 9, (sibling, code))
    u_far.start()

    wait_bytes(w_all.at[others], recv_sem.at[8])
    w_tile = w_all[...].reshape(tokens, LANES)
    x_tile = x_all[...].reshape(tokens, LANES)
    errors = (dot(w_tile, cmap[...]) - x_tile.astype(F32)).astype(BF16)
    g_buf[...] = dot(w_tile, errors, TN) * (1.0 / math.sqrt(tokens))
    g_out = pltpu.make_async_copy(g_buf, g_ref, out_sem.at[1])
    g_out.start()

    wait_bytes(x_all.at[pl.ds(0, 3)], send_sem.at[0])
    for g in range(1, len(NEAR)):
        wait_bytes(x_all.at[pl.ds(0, 4)], send_sem.at[g])
    wait_bytes(lse.at[others], send_sem.at[4])
    wait_bytes(w_send.at[others], send_sem.at[5])
    pair.wait_send()
    wait_bytes(u_all.at[pl.ds(0, len(spots))], send_sem.at[7])
    wait_bytes(w_all.at[others], send_sem.at[8])
    q_out.wait()
    u_copy.wait()
    u_far.wait()
    g_out.wait()


def deliver(q_in, u_in, g_in, q_ref, u_ref, g_ref, sem):
    copies = [
        pltpu.make_async_copy(src, dst, sem.at[i])
        for i, (src, dst) in enumerate(((g_in, g_ref), (u_in, u_ref), (q_in, q_ref)))
    ]
    for copy in copies:
        copy.start()
    for copy in copies:
        copy.wait()


def body(n_dp, n_code, latents, basis, code_map):
    rows, width = latents.shape
    codes = basis.shape[0]
    nblk = codes // CHUNK
    tokens = rows * n_code
    half = codes // 2
    vm = pltpu.VMEM
    anywhere = pl.BlockSpec(memory_space=pl.ANY)
    quantized, usage, grad = pl.pallas_call(
        functools.partial(kernel, n_dp, n_code),
        out_shape=(
            jax.ShapeDtypeStruct((rows, width), BF16),
            jax.ShapeDtypeStruct((2, half // LANES, LANES), F32),
            jax.ShapeDtypeStruct((width, width), F32),
        ),
        in_specs=[pl.BlockSpec(memory_space=pltpu.HBM)] * 3,
        out_specs=[anywhere] * 3,
        scratch_shapes=[
            vm((codes, width), BF16),
            vm((width, width), BF16),
            vm((codes, width), BF16),
            vm((8, codes), F32),
            vm((n_code, rows, width), BF16),
            vm((LANES, codes), F32),
            vm((tokens, codes), BF16),
            vm((tokens, LANES), F32),
            vm((tokens, LANES), F32),
            vm((n_code, 2 * tokens // LANES, LANES), F32),
            vm((n_code, rows, width), BF16),
            vm((n_code, rows, width), BF16),
            vm((tokens // LANES, LANES, LANES), F32),
            vm((n_code, rows, width), BF16),
            vm((rows, width), BF16),
            vm((width, width), F32),
            vm((half // LANES, LANES), F32),
            vm((half // LANES, LANES), F32),
            vm((half // LANES, LANES), F32),
            vm((n_dp // 2, half // LANES, LANES), BF16),
            vm((half // LANES, LANES), F32),
            pltpu.SemaphoreType.DMA((nblk + 2,)),
            pltpu.SemaphoreType.DMA((3,)),
            pltpu.SemaphoreType.DMA((10,)),
            pltpu.SemaphoreType.DMA((10,)),
        ],
        compiler_params=pltpu.CompilerParams(
            collective_id=0, has_side_effects=True, vmem_limit_bytes=40 * 1024 * 1024
        ),
    )(latents, basis, code_map)
    return pl.pallas_call(
        deliver,
        out_shape=(
            jax.ShapeDtypeStruct((rows, width), BF16),
            jax.ShapeDtypeStruct((codes,), F32),
            jax.ShapeDtypeStruct((width, width), F32),
        ),
        in_specs=[anywhere] * 3,
        out_specs=[anywhere] * 3,
        scratch_shapes=[pltpu.SemaphoreType.DMA((3,))],
    )(quantized, usage.reshape(codes), grad)


def solution(mesh):
    return jax.shard_map(
        functools.partial(body, mesh.shape["dp"], mesh.shape["code"]),
        mesh=mesh,
        in_specs=(P(("dp", "code"), None), P("code", None), P()),
        out_specs=(P(("dp", "code"), None), P("code"), P("dp", None)),
        check_vma=False,
    )
```

```python
import functools
import math

import jax
import jax.numpy as jnp
from jax import lax
from jax.experimental import pallas as pl
from jax.experimental.pallas import tpu as pltpu
from jax.sharding import PartitionSpec as P

MESH = pl.DeviceIdType.MESH
F32 = jnp.float32
BF16 = jnp.bfloat16
NN = (((1,), (0,)), ((), ()))
NT = (((1,), (1,)), ((), ()))
TN = (((0,), (0,)), ((), ()))
LANES = 128
CHUNK = 2048

RING = 8
NEAR = (
    ((0, 0), (0, 1), (0, 7), (1, 0), (0, 2), (0, 6), (1, 1), (1, 7)),
    ((0, 3), (0, 5), (1, 2), (1, 6), (0, 4), (1, 3), (1, 5), (1, 4)),
)
X = 4
ZH = 4


def dot(a, b, dims=NN):
    return lax.dot_general(a, b, dims, preferred_element_type=F32)


def split_three(values):
    upper = values.astype(BF16)
    rest = values - upper.astype(F32)
    middle = rest.astype(BF16)
    lower = (rest - middle.astype(F32)).astype(BF16)
    return (upper, middle, lower)


def wide(column, width):
    return jnp.concatenate([column] * (width // LANES), axis=1)


def wait_bytes(ref, sem):
    pltpu.make_async_copy(ref, ref, sem).wait()


def make_codebook(i, bas, cmap, cb, sq):
    part = slice(i * CHUNK, (i + 1) * CHUNK)
    code = dot(bas[part, :], cmap[...]).astype(BF16)
    cb[part, :] = code
    wide_code = code.astype(F32)
    square = wide_code * wide_code
    upper = square.astype(BF16)
    lower = (square - upper.astype(F32)).astype(BF16)
    ones = jnp.full((16, 2 * LANES), -0.0625, BF16)
    total = dot(ones, jnp.concatenate([upper, lower], axis=1), NT)
    sq[:, part] = total[:8]


def group_scores(x_group, cb, sq, s_buf, top):
    codes = cb.shape[0]
    s = dot(x_group[...], cb[...], NT) + sq[0:1, :]
    s_buf[...] = s
    best = s[:, :LANES]
    for j in range(1, codes // LANES):
        best = jnp.maximum(best, s[:, j * LANES:(j + 1) * LANES])
    top[...] = jnp.broadcast_to(jnp.max(best, axis=1, keepdims=True), best.shape)


def group_weights(part, s_buf, top, bas, w_buf, acc):
    codes = bas.shape[0]
    w = jnp.exp(s_buf[...] - wide(top[...], codes)).astype(BF16)
    w_buf[part, :] = w
    acc[...] = dot(w, jnp.concatenate([bas[...], jnp.ones((codes, LANES), BF16)], axis=1))


def lanes_of(columns):
    rows = columns.shape[0]
    eye = lax.broadcasted_iota(jnp.int32, (LANES, LANES), 0) == lax.broadcasted_iota(
        jnp.int32, (LANES, LANES), 1
    )
    out = []
    for g in range(rows // LANES):
        part = jnp.where(eye, columns[g * LANES:(g + 1) * LANES], 0.0)
        out.append(jnp.sum(part, axis=0, keepdims=True))
    return jnp.concatenate(out, axis=0)


def usage_half(r3, w_buf, start, out):
    width = w_buf.shape[1] // 2
    u = jnp.sum(dot(r3, w_buf[:, pl.ds(start, width)]), axis=0, keepdims=True)
    for j in range(width // LANES):
        out[j:j + 1, :] = u[:, j * LANES:(j + 1) * LANES]


def kernel(n_dp, n_code, x_ref, basis_ref, map_ref, q_ref, u_ref, g_ref,
           bas, cmap, cb, sq, x_all, x_group, order, s_buf, top, w_buf, acc, m_col, t_col,
           lse, w_send, w_recv, fac, w_all, q_buf, g_buf,
           u_send, u_mine, u_pair, u_all, u_out,
           load_sem, out_sem, send_sem, recv_sem):
    dp = lax.axis_index("dp")
    code = lax.axis_index("code")
    z_lo, y = code // RING, lax.rem(code, RING)
    core = lax.rem(dp, 2)
    x_pos = lax.rem(dp // 2, X)
    z_hi = dp // (2 * X)
    spot = dp // 2
    codes = basis_ref.shape[0]
    nblk = codes // CHUNK
    rows = x_ref.shape[0]
    tokens = rows * n_code
    groups = tokens // LANES

    def peer_code(offset):
        return lax.rem(z_lo + offset[0], n_code // RING) * RING + lax.rem(y + offset[1], RING)

    owners = [[peer_code(o) for o in group] for group in NEAR]
    far_first = [p for group in reversed(owners) for p in reversed(group)][:-1]
    sibling = dp + 1 - 2 * core
    spots = [
        (lax.rem(z_hi + a, ZH) * X + lax.rem(x_pos + b, X)) * 2 + core
        for a in (2, 1, 3, 0) for b in (2, 1, 3, 0)
    ][:-1]

    x_load = pltpu.make_async_copy(x_ref, x_all.at[code], load_sem.at[nblk])
    m_load = pltpu.make_async_copy(map_ref, cmap, load_sem.at[nblk + 1])
    b_loads = [
        pltpu.make_async_copy(
            basis_ref.at[pl.ds(i * CHUNK, CHUNK)], bas.at[pl.ds(i * CHUNK, CHUNK)], load_sem.at[i]
        )
        for i in range(nblk)
    ]
    x_load.start()
    m_load.start()
    for load in b_loads:
        load.start()

    barrier = pltpu.get_barrier_semaphore()
    for p in far_first:
        pl.semaphore_signal(barrier, inc=1, device_id=(dp, p), device_id_type=MESH)
    for d in spots + [sibling]:
        pl.semaphore_signal(barrier, inc=1, device_id=(d, code), device_id_type=MESH)

    def remote(src, dst, phase, device):
        return pltpu.make_async_remote_copy(
            src_ref=src, dst_ref=dst, send_sem=send_sem.at[phase], recv_sem=recv_sem.at[phase],
            device_id=device, device_id_type=MESH,
        )

    x_load.wait()
    m_load.wait()
    pl.semaphore_wait(barrier, len(far_first) + len(spots) + 1)

    def send_sums(g):
        for p, offset in zip(reversed(owners[g]), reversed(NEAR[g])):
            if offset != (0, 0):
                remote(w_send.at[p], w_recv.at[code], 3, (dp, p)).start()

    for g in reversed(range(len(NEAR))):
        for p, offset in zip(owners[g], NEAR[g]):
            if offset != (0, 0):
                remote(x_all.at[code], x_all.at[code], g, (dp, p)).start()

    by_distance = [o for group in owners for o in group]
    lane = lax.broadcasted_iota(jnp.int32, (1, LANES), 1)
    per = LANES // rows
    target = []
    for g in range(groups):
        owner = jnp.full((1, LANES), by_distance[g * per])
        for j in range(1, per):
            owner = jnp.where(lane >= j * rows, by_distance[g * per + j], owner)
        target.append(owner * rows + lax.rem(lane, rows))
    target = jnp.broadcast_to(jnp.concatenate(target, axis=1), (tokens, tokens))
    hit = lax.broadcasted_iota(jnp.int32, (tokens, tokens), 0) == target
    order[...] = jnp.where(hit, 1.0, 0.0).astype(BF16)

    for i in range(nblk):
        b_loads[i].wait()
        make_codebook(i, bas, cmap, cb, sq)

    always = lax.rem(dp * (dp + 1), 2) == 0
    for g, group in enumerate(owners):
        size = len(group) * rows
        arriving = len(group) - (1 if g == 0 else 0)
        wait_bytes(x_all.at[pl.ds(0, arriving)], recv_sem.at[g])
        for j, o in enumerate(group):
            x_group[j * rows:(j + 1) * rows, :] = x_all[o] * jnp.asarray(0.125, BF16)
        group_scores(x_group, cb, sq, s_buf, top)
        part = slice(g * size, (g + 1) * size)
        pl.when(always)(lambda: group_weights(part, s_buf, top, bas, w_buf, acc))
        for j, o in enumerate(group):
            part = slice(j * rows, (j + 1) * rows)
            place = pl.ds(pl.multiple_of(o * rows, rows), rows)
            m_col[place, :] = top[part, :]
            t_col[place, :] = acc[part, LANES:]
            w_send[o] = acc[part, :LANES].astype(BF16)
        if g == 0:
            send_sums(0)

    lse[code] = jnp.concatenate([lanes_of(m_col[...]), lanes_of(t_col[...])], axis=0)
    for p in far_first:
        remote(lse.at[code], lse.at[code], 2, (dp, p)).start()
    send_sums(1)
    w_recv[code] = w_send[code]

    others = pl.ds(0, n_code - 1)
    wait_bytes(lse.at[others], recv_sem.at[2])
    tops = lse[:, :groups, :]
    best = jnp.max(tops, axis=0)
    factor = jnp.exp(tops - best[None])
    total = jnp.sum(factor * lse[:, groups:, :], axis=0)
    own = jnp.exp(lse[code, :groups, :] - best) / total
    own_row = jnp.concatenate([own[g:g + 1] for g in range(groups)], axis=1)
    place = lax.broadcasted_iota(jnp.int32, (16, tokens), 0)
    r3 = jnp.zeros((16, tokens), F32)
    for j, piece in enumerate(split_three(own_row)):
        r3 = jnp.where(place == j, jnp.broadcast_to(piece.astype(F32), r3.shape), r3)
    r3 = dot(r3.astype(BF16), order[...]).astype(BF16)

    half = codes // 2
    usage_half(r3, w_buf, pl.multiple_of((1 - core) * half, half), u_send)
    pair = remote(u_send, u_pair, 4, (sibling, code))
    pair.start()
    usage_half(r3, w_buf, pl.multiple_of(core * half, half), u_mine)
    pair.wait_recv()
    u_all[spot] = (u_mine[...] + u_pair[...]).astype(BF16)
    for d in spots:
        remote(u_all.at[spot], u_all.at[spot], 5, (d, code)).start()

    scaled = factor / total[None]
    for g in range(groups):
        fac[g, :n_code] = scaled[:, g, :]
        fac[g, n_code:] = jnp.zeros((LANES - n_code, LANES), F32)
    fac[0] = jnp.transpose(fac[code // per])
    mine = fac[0, pl.ds(pl.multiple_of(lax.rem(code, per) * rows, rows), rows), :]

    wait_bytes(w_recv.at[others], recv_sem.at[3])
    w_own = jnp.zeros((rows, LANES), F32)
    for c in range(n_code):
        w_own = w_own + mine[:, c:c + 1] * w_recv[c].astype(F32)
    w_all[code] = w_own.astype(BF16)
    for p in far_first:
        remote(w_all.at[code], w_all.at[code], 6, (dp, p)).start()

    soft_own = jnp.zeros((rows, LANES), F32)
    for piece in split_three(w_own):
        soft_own = soft_own + dot(piece, cmap[...])
    q_buf[...] = soft_own.astype(BF16)
    q_out = pltpu.make_async_copy(q_buf, q_ref, out_sem.at[0])
    q_out.start()

    wait_bytes(u_all.at[pl.ds(0, len(spots))], recv_sem.at[5])
    scale = (codes * n_code) / (tokens * n_dp)
    u_out[...] = jnp.sum(u_all[...].astype(F32), axis=0) * scale
    u_copy = pltpu.make_async_copy(u_out, u_ref.at[core], out_sem.at[2])
    u_copy.start()
    u_far = remote(u_out, u_ref.at[core], 7, (sibling, code))
    u_far.start()

    wait_bytes(w_all.at[others], recv_sem.at[6])
    w_tile = w_all[...].reshape(tokens, LANES)
    x_tile = x_all[...].reshape(tokens, LANES)
    errors = (dot(w_tile, cmap[...]) - x_tile.astype(F32)).astype(BF16)
    g_buf[...] = dot(w_tile, errors, TN) * (1.0 / math.sqrt(tokens))
    g_out = pltpu.make_async_copy(g_buf, g_ref, out_sem.at[1])
    g_out.start()

    wait_bytes(x_all.at[pl.ds(0, len(NEAR[0]) - 1)], send_sem.at[0])
    wait_bytes(x_all.at[pl.ds(0, len(NEAR[1]))], send_sem.at[1])
    wait_bytes(lse.at[others], send_sem.at[2])
    wait_bytes(w_send.at[others], send_sem.at[3])
    pair.wait_send()
    wait_bytes(u_all.at[pl.ds(0, len(spots))], send_sem.at[5])
    wait_bytes(w_all.at[others], send_sem.at[6])
    q_out.wait()
    u_copy.wait()
    u_far.wait()
    g_out.wait()


def deliver(q_in, u_in, g_in, q_ref, u_ref, g_ref, sem):
    copies = [
        pltpu.make_async_copy(src, dst, sem.at[i])
        for i, (src, dst) in enumerate(((g_in, g_ref), (u_in, u_ref), (q_in, q_ref)))
    ]
    for copy in copies:
        copy.start()
    for copy in copies:
        copy.wait()


def body(n_dp, n_code, latents, basis, code_map):
    rows, width = latents.shape
    codes = basis.shape[0]
    nblk = codes // CHUNK
    tokens = rows * n_code
    half = codes // 2
    vm = pltpu.VMEM
    anywhere = pl.BlockSpec(memory_space=pl.ANY)
    quantized, usage, grad = pl.pallas_call(
        functools.partial(kernel, n_dp, n_code),
        out_shape=(
            vm((rows, width), BF16),
            vm((2, half // LANES, LANES), F32),
            vm((width, width), F32),
        ),
        in_specs=[pl.BlockSpec(memory_space=pltpu.HBM)] * 3,
        out_specs=[anywhere] * 3,
        scratch_shapes=[
            vm((codes, width), BF16),
            vm((width, width), BF16),
            vm((codes, width), BF16),
            vm((8, codes), F32),
            vm((n_code, rows, width), BF16),
            vm((tokens // 2, width), BF16),
            vm((tokens, tokens), BF16),
            vm((tokens // 2, codes), F32),
            vm((tokens // 2, LANES), F32),
            vm((tokens, codes), BF16),
            vm((tokens // 2, 2 * width), F32),
            vm((tokens, LANES), F32),
            vm((tokens, LANES), F32),
            vm((n_code, 2 * tokens // LANES, LANES), F32),
            vm((n_code, rows, width), BF16),
            vm((n_code, rows, width), BF16),
            vm((tokens // LANES, LANES, LANES), F32),
            vm((n_code, rows, width), BF16),
            vm((rows, width), BF16),
            vm((width, width), F32),
            vm((half // LANES, LANES), F32),
            vm((half // LANES, LANES), F32),
            vm((half // LANES, LANES), F32),
            vm((n_dp // 2, half // LANES, LANES), BF16),
            vm((half // LANES, LANES), F32),
            pltpu.SemaphoreType.DMA((nblk + 2,)),
            pltpu.SemaphoreType.DMA((3,)),
            pltpu.SemaphoreType.DMA((8,)),
            pltpu.SemaphoreType.DMA((8,)),
        ],
        compiler_params=pltpu.CompilerParams(
            collective_id=0, has_side_effects=True, vmem_limit_bytes=40 * 1024 * 1024
        ),
    )(*(pltpu.with_memory_space_constraint(a, pltpu.HBM) for a in (latents, basis, code_map)))
    return pl.pallas_call(
        deliver,
        out_shape=(
            jax.ShapeDtypeStruct((rows, width), BF16),
            jax.ShapeDtypeStruct((codes,), F32),
            jax.ShapeDtypeStruct((width, width), F32),
        ),
        in_specs=[anywhere] * 3,
        out_specs=[anywhere] * 3,
        scratch_shapes=[pltpu.SemaphoreType.DMA((3,))],
    )(*(pltpu.with_memory_space_constraint(a, vm) for a in (quantized, usage.reshape(codes), grad)))


def solution(mesh):
    return jax.shard_map(
        functools.partial(body, mesh.shape["dp"], mesh.shape["code"]),
        mesh=mesh,
        in_specs=(P(("dp", "code"), None), P("code", None), P()),
        out_specs=(P(("dp", "code"), None), P("code"), P("dp", None)),
        check_vma=False,
    )
```

```python
import functools
import math

import jax
import jax.numpy as jnp
from jax import lax
from jax.experimental import pallas as pl
from jax.experimental.pallas import tpu as pltpu
from jax.sharding import PartitionSpec as P

MESH = pl.DeviceIdType.MESH
F32 = jnp.float32
BF16 = jnp.bfloat16
NN = (((1,), (0,)), ((), ()))
NT = (((1,), (1,)), ((), ()))
TN = (((0,), (0,)), ((), ()))
LANES = 128
CHUNK = 2048

RING = 8
NEAR = (
    ((0, 0), (0, 1), (0, 7), (1, 0), (0, 2), (0, 6), (1, 1), (1, 7)),
    ((1, 4), (0, 4), (1, 3), (1, 5), (0, 3), (0, 5), (1, 2), (1, 6)),
)
X = 4
ZH = 4


def dot(a, b, dims=NN):
    return lax.dot_general(a, b, dims, preferred_element_type=F32)


def split_three(values):
    upper = values.astype(BF16)
    rest = values - upper.astype(F32)
    middle = rest.astype(BF16)
    lower = (rest - middle.astype(F32)).astype(BF16)
    return (upper, middle, lower)


def wide(column, width):
    return jnp.concatenate([column] * (width // LANES), axis=1)


def wait_bytes(ref, sem):
    pltpu.make_async_copy(ref, ref, sem).wait()


def make_codebook(i, bas, cmap, cb, sq):
    part = slice(i * CHUNK, (i + 1) * CHUNK)
    code = dot(bas[part, :], cmap[...]).astype(BF16)
    cb[part, :] = code
    wide_code = code.astype(F32)
    square = wide_code * wide_code
    upper = square.astype(BF16)
    lower = (square - upper.astype(F32)).astype(BF16)
    ones = jnp.full((16, 2 * LANES), -0.0625, BF16)
    total = dot(ones, jnp.concatenate([upper, lower], axis=1), NT)
    sq[:, part] = total[:8]


def group_scores(x_group, cb, sq, s_buf, top):
    codes = cb.shape[0]
    s = dot(x_group[...], cb[...], NT) + sq[0:1, :]
    s_buf[...] = s
    best = s[:, :LANES]
    for j in range(1, codes // LANES):
        best = jnp.maximum(best, s[:, j * LANES:(j + 1) * LANES])
    top[...] = jnp.broadcast_to(jnp.max(best, axis=1, keepdims=True), best.shape)


def group_weights(part, s_buf, top, bas, w_buf, acc):
    codes = bas.shape[0]
    w = jnp.exp(s_buf[...] - wide(top[...], codes)).astype(BF16)
    w_buf[part, :] = w
    acc[...] = dot(w, jnp.concatenate([bas[...], jnp.ones((codes, LANES), BF16)], axis=1))


def lanes_of(columns):
    rows = columns.shape[0]
    eye = lax.broadcasted_iota(jnp.int32, (LANES, LANES), 0) == lax.broadcasted_iota(
        jnp.int32, (LANES, LANES), 1
    )
    out = []
    for g in range(rows // LANES):
        part = jnp.where(eye, columns[g * LANES:(g + 1) * LANES], 0.0)
        out.append(jnp.sum(part, axis=0, keepdims=True))
    return jnp.concatenate(out, axis=0)


def usage_half(r3, w_buf, start, out):
    width = w_buf.shape[1] // 2
    u = jnp.sum(dot(r3, w_buf[:, pl.ds(start, width)]), axis=0, keepdims=True)
    for j in range(width // LANES):
        out[j:j + 1, :] = u[:, j * LANES:(j + 1) * LANES]


def kernel(n_dp, n_code, x_ref, basis_ref, map_ref, q_ref, u_ref, g_ref,
           bas, cmap, cb, sq, x_all, x_group, order, s_buf, top, w_buf, acc, m_col, t_col,
           lse, w_send, w_recv, fac, w_all, q_buf, g_buf,
           u_row, u_send, u_level, u_all, u_out,
           load_sem, out_sem, send_sem, recv_sem):
    dp = lax.axis_index("dp")
    code = lax.axis_index("code")
    z_lo, y = code // RING, lax.rem(code, RING)
    core = lax.rem(dp, 2)
    x_pos = lax.rem(dp // 2, X)
    z_hi = dp // (2 * X)
    codes = basis_ref.shape[0]
    nblk = codes // CHUNK
    rows = x_ref.shape[0]
    tokens = rows * n_code
    groups = tokens // LANES

    def peer_code(offset):
        return lax.rem(z_lo + offset[0], n_code // RING) * RING + lax.rem(y + offset[1], RING)

    owners = [[peer_code(o) for o in group] for group in NEAR]
    far_first = owners[1] + owners[0][:0:-1]
    rank = lax.rem(dp, 2 * X)

    def peer_dp(a, b, c):
        return (lax.rem(z_hi + a, ZH) * X + lax.rem(x_pos + b, X)) * 2 + c

    level_other = [peer_dp(0, b, 1 - core) for b in (2, 1, 3, 0)]
    level_same = [peer_dp(0, b, core) for b in (2, 1, 3)]
    column = [peer_dp(a, 0, c) for a in (2, 1, 3) for c in (core, 1 - core)]

    x_load = pltpu.make_async_copy(x_ref, x_all.at[code], load_sem.at[nblk])
    m_load = pltpu.make_async_copy(map_ref, cmap, load_sem.at[nblk + 1])
    b_loads = [
        pltpu.make_async_copy(
            basis_ref.at[pl.ds(i * CHUNK, CHUNK)], bas.at[pl.ds(i * CHUNK, CHUNK)], load_sem.at[i]
        )
        for i in range(nblk)
    ]
    x_load.start()
    m_load.start()
    for load in b_loads:
        load.start()

    barrier = pltpu.get_barrier_semaphore()
    for p in far_first:
        pl.semaphore_signal(barrier, inc=1, device_id=(dp, p), device_id_type=MESH)
    for d in column + level_other + level_same:
        pl.semaphore_signal(barrier, inc=1, device_id=(d, code), device_id_type=MESH)

    def remote(src, dst, phase, device):
        return pltpu.make_async_remote_copy(
            src_ref=src, dst_ref=dst, send_sem=send_sem.at[phase], recv_sem=recv_sem.at[phase],
            device_id=device, device_id_type=MESH,
        )

    x_load.wait()
    m_load.wait()
    pl.semaphore_wait(barrier, n_code - 1 + len(column + level_other + level_same))

    def send_sums(g):
        for p, offset in zip(owners[g], NEAR[g]):
            if offset != (0, 0):
                remote(w_send.at[p], w_recv.at[code], 3, (dp, p)).start()

    for g in range(len(NEAR)):
        for p, offset in zip(owners[g], NEAR[g]):
            if offset != (0, 0):
                remote(x_all.at[code], x_all.at[code], g, (dp, p)).start()

    by_distance = [o for group in owners for o in group]
    lane = lax.broadcasted_iota(jnp.int32, (1, LANES), 1)
    per = LANES // rows
    target = []
    for g in range(groups):
        owner = jnp.full((1, LANES), by_distance[g * per])
        for j in range(1, per):
            owner = jnp.where(lane >= j * rows, by_distance[g * per + j], owner)
        target.append(owner * rows + lax.rem(lane, rows))
    target = jnp.broadcast_to(jnp.concatenate(target, axis=1), (tokens, tokens))
    hit = lax.broadcasted_iota(jnp.int32, (tokens, tokens), 0) == target
    order[...] = jnp.where(hit, 1.0, 0.0).astype(BF16)

    for i in range(nblk):
        b_loads[i].wait()
        make_codebook(i, bas, cmap, cb, sq)

    always = lax.rem(dp * (dp + 1), 2) == 0
    for g, group in enumerate(owners):
        size = len(group) * rows
        arriving = len(group) - (1 if g == 0 else 0)
        wait_bytes(x_all.at[pl.ds(0, arriving)], recv_sem.at[g])
        for j, o in enumerate(group):
            x_group[j * rows:(j + 1) * rows, :] = x_all[o] * jnp.asarray(0.125, BF16)
        group_scores(x_group, cb, sq, s_buf, top)
        part = slice(g * size, (g + 1) * size)
        pl.when(always)(lambda: group_weights(part, s_buf, top, bas, w_buf, acc))
        for j, o in enumerate(group):
            part = slice(j * rows, (j + 1) * rows)
            place = pl.ds(pl.multiple_of(o * rows, rows), rows)
            m_col[place, :] = top[part, :]
            t_col[place, :] = acc[part, LANES:]
            w_send[o] = acc[part, :LANES].astype(BF16)
        if g == 0:
            send_sums(0)

    lse[code] = jnp.concatenate([lanes_of(m_col[...]), lanes_of(t_col[...])], axis=0)
    for p in far_first:
        remote(lse.at[code], lse.at[code], 2, (dp, p)).start()
    send_sums(1)
    w_recv[code] = w_send[code]

    others = pl.ds(0, n_code - 1)
    wait_bytes(lse.at[others], recv_sem.at[2])
    tops = lse[:, :groups, :]
    best = jnp.max(tops, axis=0)
    factor = jnp.exp(tops - best[None])
    total = jnp.sum(factor * lse[:, groups:, :], axis=0)
    own = jnp.exp(lse[code, :groups, :] - best) / total
    own_row = jnp.concatenate([own[g:g + 1] for g in range(groups)], axis=1)
    place = lax.broadcasted_iota(jnp.int32, (16, tokens), 0)
    r3 = jnp.zeros((16, tokens), F32)
    for j, piece in enumerate(split_three(own_row)):
        r3 = jnp.where(place == j, jnp.broadcast_to(piece.astype(F32), r3.shape), r3)
    r3 = dot(r3.astype(BF16), order[...]).astype(BF16)

    half = codes // 2
    usage_half(r3, w_buf, pl.multiple_of((1 - core) * half, half), u_row)
    u_send[0] = u_row[...].astype(BF16)
    for d in level_other:
        remote(u_send.at[0], u_level.at[rank], 4, (d, code)).start()
    usage_half(r3, w_buf, pl.multiple_of(core * half, half), u_row)
    u_send[1] = u_row[...].astype(BF16)
    for d in level_same:
        remote(u_send.at[1], u_level.at[rank], 4, (d, code)).start()
    u_level[rank] = u_send[1]

    scaled = factor / total[None]
    for g in range(groups):
        fac[g, :n_code] = scaled[:, g, :]
        fac[g, n_code:] = jnp.zeros((LANES - n_code, LANES), F32)
    fac[0] = jnp.transpose(fac[code // per])
    mine = fac[0, pl.ds(pl.multiple_of(lax.rem(code, per) * rows, rows), rows), :]

    wait_bytes(w_recv.at[others], recv_sem.at[3])
    w_own = jnp.zeros((rows, LANES), F32)
    for c in range(n_code):
        w_own = w_own + mine[:, c:c + 1] * w_recv[c].astype(F32)
    w_all[code] = w_own.astype(BF16)
    for p in far_first:
        remote(w_all.at[code], w_all.at[code], 6, (dp, p)).start()

    soft_own = jnp.zeros((rows, LANES), F32)
    for piece in split_three(w_own):
        soft_own = soft_own + dot(piece, cmap[...])
    q_buf[...] = soft_own.astype(BF16)
    q_out = pltpu.make_async_copy(q_buf, q_ref, out_sem.at[0])
    q_out.start()

    level = pl.ds(0, len(level_other + level_same))
    wait_bytes(u_level.at[level], recv_sem.at[4])
    u_all[z_hi, core] = jnp.sum(u_level[...].astype(F32), axis=0).astype(BF16)
    last = peer_dp(0, 0, 1 - core)
    for d in column + [last]:
        remote(u_all.at[z_hi, core], u_all.at[z_hi, core], 5, (d, code)).start()

    wait_bytes(w_all.at[others], recv_sem.at[6])
    w_tile = w_all[...].reshape(tokens, LANES)
    x_tile = x_all[...].reshape(tokens, LANES)
    errors = (dot(w_tile, cmap[...]) - x_tile.astype(F32)).astype(BF16)
    g_buf[...] = dot(w_tile, errors, TN) * (1.0 / math.sqrt(tokens))
    g_out = pltpu.make_async_copy(g_buf, g_ref, out_sem.at[1])
    g_out.start()

    wait_bytes(u_level.at[level], recv_sem.at[5])
    scale = (codes * n_code) / (tokens * n_dp)
    u_out[...] = jnp.sum(u_all[...].astype(F32), axis=0) * scale
    u_copy = pltpu.make_async_copy(u_out, u_ref, out_sem.at[2])
    u_copy.start()

    wait_bytes(x_all.at[pl.ds(0, len(NEAR[0]) - 1)], send_sem.at[0])
    wait_bytes(x_all.at[pl.ds(0, len(NEAR[1]))], send_sem.at[1])
    wait_bytes(lse.at[others], send_sem.at[2])
    wait_bytes(w_send.at[others], send_sem.at[3])
    wait_bytes(u_level.at[level], send_sem.at[4])
    wait_bytes(u_level.at[level], send_sem.at[5])
    wait_bytes(w_all.at[others], send_sem.at[6])
    q_out.wait()
    u_copy.wait()
    g_out.wait()


def deliver(q_in, u_in, g_in, q_ref, u_ref, g_ref, sem):
    copies = [
        pltpu.make_async_copy(src, dst, sem.at[i])
        for i, (src, dst) in enumerate(((g_in, g_ref), (u_in, u_ref), (q_in, q_ref)))
    ]
    for copy in copies:
        copy.start()
    for copy in copies:
        copy.wait()


def body(n_dp, n_code, latents, basis, code_map):
    rows, width = latents.shape
    codes = basis.shape[0]
    nblk = codes // CHUNK
    tokens = rows * n_code
    half = codes // 2
    vm = pltpu.VMEM
    anywhere = pl.BlockSpec(memory_space=pl.ANY)
    quantized, usage, grad = pl.pallas_call(
        functools.partial(kernel, n_dp, n_code),
        out_shape=(
            vm((rows, width), BF16),
            vm((2, half // LANES, LANES), F32),
            vm((width, width), F32),
        ),
        in_specs=[pl.BlockSpec(memory_space=pltpu.HBM)] * 3,
        out_specs=[anywhere] * 3,
        scratch_shapes=[
            vm((codes, width), BF16),
            vm((width, width), BF16),
            vm((codes, width), BF16),
            vm((8, codes), F32),
            vm((n_code, rows, width), BF16),
            vm((tokens // 2, width), BF16),
            vm((tokens, tokens), BF16),
            vm((tokens // 2, codes), F32),
            vm((tokens // 2, LANES), F32),
            vm((tokens, codes), BF16),
            vm((tokens // 2, 2 * width), F32),
            vm((tokens, LANES), F32),
            vm((tokens, LANES), F32),
            vm((n_code, 2 * tokens // LANES, LANES), F32),
            vm((n_code, rows, width), BF16),
            vm((n_code, rows, width), BF16),
            vm((tokens // LANES, LANES, LANES), F32),
            vm((n_code, rows, width), BF16),
            vm((rows, width), BF16),
            vm((width, width), F32),
            vm((half // LANES, LANES), F32),
            vm((2, half // LANES, LANES), BF16),
            vm((2 * X, half // LANES, LANES), BF16),
            vm((ZH, 2, half // LANES, LANES), BF16),
            vm((2, half // LANES, LANES), F32),
            pltpu.SemaphoreType.DMA((nblk + 2,)),
            pltpu.SemaphoreType.DMA((3,)),
            pltpu.SemaphoreType.DMA((7,)),
            pltpu.SemaphoreType.DMA((7,)),
        ],
        compiler_params=pltpu.CompilerParams(
            collective_id=0, has_side_effects=True, vmem_limit_bytes=40 * 1024 * 1024
        ),
    )(*(pltpu.with_memory_space_constraint(a, pltpu.HBM) for a in (latents, basis, code_map)))
    return pl.pallas_call(
        deliver,
        out_shape=(
            jax.ShapeDtypeStruct((rows, width), BF16),
            jax.ShapeDtypeStruct((codes,), F32),
            jax.ShapeDtypeStruct((width, width), F32),
        ),
        in_specs=[anywhere] * 3,
        out_specs=[anywhere] * 3,
        scratch_shapes=[pltpu.SemaphoreType.DMA((3,))],
    )(*(pltpu.with_memory_space_constraint(a, vm) for a in (quantized, usage.reshape(codes), grad)))


def solution(mesh):
    return jax.shard_map(
        functools.partial(body, mesh.shape["dp"], mesh.shape["code"]),
        mesh=mesh,
        in_specs=(P(("dp", "code"), None), P("code", None), P()),
        out_specs=(P(("dp", "code"), None), P("code"), P("dp", None)),
        check_vma=False,
    )
```

```python
import functools
import math

import jax
import jax.numpy as jnp
from jax import lax
from jax.experimental import pallas as pl
from jax.experimental.pallas import tpu as pltpu
from jax.sharding import PartitionSpec as P

MESH = pl.DeviceIdType.MESH
F32 = jnp.float32
BF16 = jnp.bfloat16
NN = (((1,), (0,)), ((), ()))
NT = (((1,), (1,)), ((), ()))
TN = (((0,), (0,)), ((), ()))
LANES = 128
CHUNK = 2048

RING = 8
NEAR = (
    ((0, 0), (0, 1), (0, 7), (1, 0)),
    ((0, 2), (0, 6), (1, 1), (1, 7)),
    ((1, 4), (0, 4), (1, 3), (1, 5), (0, 3), (0, 5), (1, 2), (1, 6)),
)
X = 4
ZH = 4


def dot(a, b, dims=NN):
    return lax.dot_general(a, b, dims, preferred_element_type=F32)


def split_three(values):
    upper = values.astype(BF16)
    rest = values - upper.astype(F32)
    middle = rest.astype(BF16)
    lower = (rest - middle.astype(F32)).astype(BF16)
    return (upper, middle, lower)


def wide(column, width):
    return jnp.concatenate([column] * (width // LANES), axis=1)


def wait_bytes(ref, sem):
    pltpu.make_async_copy(ref, ref, sem).wait()


def make_codebook(i, bas, cmap, cb, sq):
    part = slice(i * CHUNK, (i + 1) * CHUNK)
    code = dot(bas[part, :], cmap[...]).astype(BF16)
    cb[part, :] = code
    wide_code = code.astype(F32)
    square = wide_code * wide_code
    upper = square.astype(BF16)
    lower = (square - upper.astype(F32)).astype(BF16)
    ones = jnp.full((16, 2 * LANES), -0.0625, BF16)
    total = dot(ones, jnp.concatenate([upper, lower], axis=1), NT)
    sq[:, part] = total[:8]


def group_scores(x_group, cb, sq, s_buf, top):
    codes = cb.shape[0]
    s = dot(x_group[...], cb[...], NT) + sq[0:1, :]
    s_buf[...] = s
    best = s[:, :LANES]
    for j in range(1, codes // LANES):
        best = jnp.maximum(best, s[:, j * LANES:(j + 1) * LANES])
    top[...] = jnp.broadcast_to(jnp.max(best, axis=1, keepdims=True), best.shape)


def group_weights(part, s_buf, top, bas, w_buf, acc):
    codes = bas.shape[0]
    w = jnp.exp(s_buf[...] - wide(top[...], codes)).astype(BF16)
    w_buf[part, :] = w
    acc[...] = dot(w, jnp.concatenate([bas[...], jnp.ones((codes, LANES), BF16)], axis=1))


def lanes_of(columns):
    rows = columns.shape[0]
    eye = lax.broadcasted_iota(jnp.int32, (LANES, LANES), 0) == lax.broadcasted_iota(
        jnp.int32, (LANES, LANES), 1
    )
    out = []
    for g in range(rows // LANES):
        part = jnp.where(eye, columns[g * LANES:(g + 1) * LANES], 0.0)
        out.append(jnp.sum(part, axis=0, keepdims=True))
    return jnp.concatenate(out, axis=0)


def usage_half(r3, w_buf, start, out):
    width = w_buf.shape[1] // 2
    u = jnp.sum(dot(r3, w_buf[:, pl.ds(start, width)]), axis=0, keepdims=True)
    for j in range(width // LANES):
        out[j:j + 1, :] = u[:, j * LANES:(j + 1) * LANES]


def kernel(n_dp, n_code, x_ref, basis_ref, map_ref, q_ref, u_ref, g_ref,
           bas, cmap, cb, sq, x_all, x_group, order, s_buf, top, w_buf, acc, m_col, t_col,
           lse, w_send, w_recv, fac, w_all,
           u_row, u_send, u_level, u_all,
           load_sem, send_sem, recv_sem):
    dp = lax.axis_index("dp")
    code = lax.axis_index("code")
    z_lo, y = code // RING, lax.rem(code, RING)
    core = lax.rem(dp, 2)
    x_pos = lax.rem(dp // 2, X)
    z_hi = dp // (2 * X)
    codes = basis_ref.shape[0]
    nblk = codes // CHUNK
    rows = x_ref.shape[0]
    tokens = rows * n_code
    groups = tokens // LANES

    def peer_code(offset):
        return lax.rem(z_lo + offset[0], n_code // RING) * RING + lax.rem(y + offset[1], RING)

    owners = [[peer_code(o) for o in group] for group in NEAR]
    far_first = owners[2] + owners[1][::-1] + owners[0][:0:-1]
    rank = lax.rem(dp, 2 * X)

    def peer_dp(a, b, c):
        return (lax.rem(z_hi + a, ZH) * X + lax.rem(x_pos + b, X)) * 2 + c

    level_other = [peer_dp(0, b, 1 - core) for b in (2, 1, 3, 0)]
    level_same = [peer_dp(0, b, core) for b in (2, 1, 3)]
    column = [peer_dp(a, 0, c) for a in (2, 1, 3) for c in (core, 1 - core)]

    x_load = pltpu.make_async_copy(x_ref, x_all.at[code], load_sem.at[nblk])
    m_load = pltpu.make_async_copy(map_ref, cmap, load_sem.at[nblk + 1])
    b_loads = [
        pltpu.make_async_copy(
            basis_ref.at[pl.ds(i * CHUNK, CHUNK)], bas.at[pl.ds(i * CHUNK, CHUNK)], load_sem.at[i]
        )
        for i in range(nblk)
    ]
    x_load.start()
    m_load.start()
    for load in b_loads:
        load.start()

    barrier = pltpu.get_barrier_semaphore()
    for p in far_first:
        pl.semaphore_signal(barrier, inc=1, device_id=(dp, p), device_id_type=MESH)
    for d in column + level_other + level_same:
        pl.semaphore_signal(barrier, inc=1, device_id=(d, code), device_id_type=MESH)

    def remote(src, dst, phase, device):
        return pltpu.make_async_remote_copy(
            src_ref=src, dst_ref=dst, send_sem=send_sem.at[phase], recv_sem=recv_sem.at[phase],
            device_id=device, device_id_type=MESH,
        )

    x_load.wait()
    m_load.wait()
    pl.semaphore_wait(barrier, n_code - 1 + len(column + level_other + level_same))

    def send_sums(g):
        for p, offset in zip(owners[g], NEAR[g]):
            if offset != (0, 0):
                remote(w_send.at[p], w_recv.at[code], 4, (dp, p)).start()

    for g in range(len(NEAR)):
        for p, offset in zip(owners[g], NEAR[g]):
            if offset != (0, 0):
                remote(x_all.at[code], x_all.at[code], g, (dp, p)).start()

    by_distance = [o for group in owners for o in group]
    lane = lax.broadcasted_iota(jnp.int32, (1, LANES), 1)
    per = LANES // rows
    target = []
    for g in range(groups):
        owner = jnp.full((1, LANES), by_distance[g * per])
        for j in range(1, per):
            owner = jnp.where(lane >= j * rows, by_distance[g * per + j], owner)
        target.append(owner * rows + lax.rem(lane, rows))
    target = jnp.broadcast_to(jnp.concatenate(target, axis=1), (tokens, tokens))
    hit = lax.broadcasted_iota(jnp.int32, (tokens, tokens), 0) == target
    order[...] = jnp.where(hit, 1.0, 0.0).astype(BF16)

    for i in range(nblk):
        b_loads[i].wait()
        make_codebook(i, bas, cmap, cb, sq)

    always = lax.rem(dp * (dp + 1), 2) == 0
    for g, group in enumerate(owners):
        size = len(group) * rows
        arriving = len(group) - (1 if g == 0 else 0)
        wait_bytes(x_all.at[pl.ds(0, arriving)], recv_sem.at[g])
        for j, o in enumerate(group):
            x_group[j * rows:(j + 1) * rows, :] = x_all[o] * jnp.asarray(0.125, BF16)
        first = sum(len(o) for o in NEAR[:g]) * rows
        part = slice(first, first + size)
        some = pl.ds(0, size)
        group_scores(x_group.at[some], cb, sq, s_buf.at[some], top.at[some])
        pl.when(always)(lambda: group_weights(part, s_buf.at[some], top.at[some], bas, w_buf, acc.at[some]))
        for j, o in enumerate(group):
            part = slice(j * rows, (j + 1) * rows)
            place = pl.ds(pl.multiple_of(o * rows, rows), rows)
            m_col[place, :] = top[part, :]
            t_col[place, :] = acc[part, LANES:]
            w_send[o] = acc[part, :LANES].astype(BF16)
        if g < 2:
            send_sums(g)

    lse[code] = jnp.concatenate([lanes_of(m_col[...]), lanes_of(t_col[...])], axis=0)
    for p in far_first:
        remote(lse.at[code], lse.at[code], 3, (dp, p)).start()
    send_sums(2)
    w_recv[code] = w_send[code]

    others = pl.ds(0, n_code - 1)
    wait_bytes(lse.at[others], recv_sem.at[3])
    tops = lse[:, :groups, :]
    best = jnp.max(tops, axis=0)
    factor = jnp.exp(tops - best[None])
    total = jnp.sum(factor * lse[:, groups:, :], axis=0)
    own = jnp.exp(lse[code, :groups, :] - best) / total
    own_row = jnp.concatenate([own[g:g + 1] for g in range(groups)], axis=1)
    place = lax.broadcasted_iota(jnp.int32, (16, tokens), 0)
    r3 = jnp.zeros((16, tokens), F32)
    for j, piece in enumerate(split_three(own_row)):
        r3 = jnp.where(place == j, jnp.broadcast_to(piece.astype(F32), r3.shape), r3)
    r3 = dot(r3.astype(BF16), order[...]).astype(BF16)

    half = codes // 2
    for k in (0, 1):
        pl.when(core == 1 - k)(lambda k=k: usage_half(r3, w_buf, k * half, u_row))
    u_send[0] = u_row[...].astype(BF16)
    for d in level_other:
        remote(u_send.at[0], u_level.at[rank], 5, (d, code)).start()
    for k in (0, 1):
        pl.when(core == k)(lambda k=k: usage_half(r3, w_buf, k * half, u_row))
    u_send[1] = u_row[...].astype(BF16)
    for d in level_same:
        remote(u_send.at[1], u_level.at[rank], 5, (d, code)).start()
    u_level[rank] = u_send[1]

    scaled = factor / total[None]
    for g in range(groups):
        fac[g, :n_code] = scaled[:, g, :]
        fac[g, n_code:] = jnp.zeros((LANES - n_code, LANES), F32)
    fac[0] = jnp.transpose(fac[code // per])
    mine = fac[0, pl.ds(pl.multiple_of(lax.rem(code, per) * rows, rows), rows), :]

    wait_bytes(w_recv.at[others], recv_sem.at[4])
    w_own = jnp.zeros((rows, LANES), F32)
    for c in range(n_code):
        w_own = w_own + mine[:, c:c + 1] * w_recv[c].astype(F32)
    w_all[code] = w_own.astype(BF16)
    for p in far_first:
        remote(w_all.at[code], w_all.at[code], 7, (dp, p)).start()

    soft_own = jnp.zeros((rows, LANES), F32)
    for piece in split_three(w_own):
        soft_own = soft_own + dot(piece, cmap[...])
    q_ref[...] = soft_own.astype(BF16)

    level = pl.ds(0, len(level_other + level_same))
    wait_bytes(u_level.at[level], recv_sem.at[5])
    u_all[z_hi, core] = jnp.sum(u_level[...].astype(F32), axis=0).astype(BF16)
    last = peer_dp(0, 0, 1 - core)
    for d in column + [last]:
        remote(u_all.at[z_hi, core], u_all.at[z_hi, core], 6, (d, code)).start()

    wait_bytes(w_all.at[others], recv_sem.at[7])
    w_tile = w_all[...].reshape(tokens, LANES)
    x_tile = x_all[...].reshape(tokens, LANES)
    errors = (dot(w_tile, cmap[...]) - x_tile.astype(F32)).astype(BF16)
    g_ref[...] = dot(w_tile, errors, TN) * (1.0 / math.sqrt(tokens))

    wait_bytes(u_level.at[level], recv_sem.at[6])
    scale = (codes * n_code) / (tokens * n_dp)
    u_ref[...] = jnp.sum(u_all[...].astype(F32), axis=0) * scale

    wait_bytes(x_all.at[pl.ds(0, len(NEAR[0]) - 1)], send_sem.at[0])
    wait_bytes(x_all.at[pl.ds(0, len(NEAR[1]))], send_sem.at[1])
    wait_bytes(x_all.at[pl.ds(0, len(NEAR[2]))], send_sem.at[2])
    wait_bytes(lse.at[others], send_sem.at[3])
    wait_bytes(w_send.at[others], send_sem.at[4])
    wait_bytes(u_level.at[level], send_sem.at[5])
    wait_bytes(u_level.at[level], send_sem.at[6])
    wait_bytes(w_all.at[others], send_sem.at[7])


def deliver(q_in, u_in, g_in, q_ref, u_ref, g_ref, sem):
    copies = [
        pltpu.make_async_copy(src, dst, sem.at[i])
        for i, (src, dst) in enumerate(((g_in, g_ref), (u_in, u_ref), (q_in, q_ref)))
    ]
    for copy in copies:
        copy.start()
    for copy in copies:
        copy.wait()


def body(n_dp, n_code, latents, basis, code_map):
    rows, width = latents.shape
    codes = basis.shape[0]
    nblk = codes // CHUNK
    tokens = rows * n_code
    half = codes // 2
    vm = pltpu.VMEM
    anywhere = pl.BlockSpec(memory_space=pl.ANY)
    quantized, usage, grad = pl.pallas_call(
        functools.partial(kernel, n_dp, n_code),
        out_shape=(
            vm((rows, width), BF16),
            vm((2, half // LANES, LANES), F32),
            vm((width, width), F32),
        ),
        in_specs=[pl.BlockSpec(memory_space=pltpu.HBM)] * 3,
        out_specs=[pl.BlockSpec(memory_space=vm)] * 3,
        scratch_shapes=[
            vm((codes, width), BF16),
            vm((width, width), BF16),
            vm((codes, width), BF16),
            vm((8, codes), F32),
            vm((n_code, rows, width), BF16),
            vm((tokens // 2, width), BF16),
            vm((tokens, tokens), BF16),
            vm((tokens // 2, codes), F32),
            vm((tokens // 2, LANES), F32),
            vm((tokens, codes), BF16),
            vm((tokens // 2, 2 * width), F32),
            vm((tokens, LANES), F32),
            vm((tokens, LANES), F32),
            vm((n_code, 2 * tokens // LANES, LANES), F32),
            vm((n_code, rows, width), BF16),
            vm((n_code, rows, width), BF16),
            vm((tokens // LANES, LANES, LANES), F32),
            vm((n_code, rows, width), BF16),
            vm((half // LANES, LANES), F32),
            vm((2, half // LANES, LANES), BF16),
            vm((2 * X, half // LANES, LANES), BF16),
            vm((ZH, 2, half // LANES, LANES), BF16),
            pltpu.SemaphoreType.DMA((nblk + 2,)),
            pltpu.SemaphoreType.DMA((8,)),
            pltpu.SemaphoreType.DMA((8,)),
        ],
        compiler_params=pltpu.CompilerParams(
            collective_id=0, has_side_effects=True, vmem_limit_bytes=40 * 1024 * 1024
        ),
    )(*(pltpu.with_memory_space_constraint(a, pltpu.HBM) for a in (latents, basis, code_map)))
    return pl.pallas_call(
        deliver,
        out_shape=(
            jax.ShapeDtypeStruct((rows, width), BF16),
            jax.ShapeDtypeStruct((codes,), F32),
            jax.ShapeDtypeStruct((width, width), F32),
        ),
        in_specs=[anywhere] * 3,
        out_specs=[anywhere] * 3,
        scratch_shapes=[pltpu.SemaphoreType.DMA((3,))],
    )(*(pltpu.with_memory_space_constraint(a, vm) for a in (quantized, usage.reshape(codes), grad)))


def solution(mesh):
    return jax.shard_map(
        functools.partial(body, mesh.shape["dp"], mesh.shape["code"]),
        mesh=mesh,
        in_specs=(P(("dp", "code"), None), P("code", None), P()),
        out_specs=(P(("dp", "code"), None), P("code"), P("dp", None)),
        check_vma=False,
    )
```

```python
import functools
import math

import jax
import jax.numpy as jnp
from jax import lax
from jax.experimental import pallas as pl
from jax.experimental.pallas import tpu as pltpu
from jax.sharding import PartitionSpec as P

MESH = pl.DeviceIdType.MESH
F32 = jnp.float32
BF16 = jnp.bfloat16
NN = (((1,), (0,)), ((), ()))
NT = (((1,), (1,)), ((), ()))
TN = (((0,), (0,)), ((), ()))
LANES = 128
CHUNK = 2048

RING = 8
NEAR = (
    ((0, 0), (0, 1), (0, 7), (1, 0)),
    ((0, 2), (0, 6), (1, 1), (1, 7)),
    ((1, 4), (0, 4), (1, 3), (1, 5), (0, 3), (0, 5), (1, 2), (1, 6)),
)
X = 4
ZH = 4


def dot(a, b, dims=NN):
    return lax.dot_general(a, b, dims, preferred_element_type=F32)


def split_three(values):
    upper = values.astype(BF16)
    rest = values - upper.astype(F32)
    middle = rest.astype(BF16)
    lower = (rest - middle.astype(F32)).astype(BF16)
    return (upper, middle, lower)


def wide(column, width):
    return jnp.concatenate([column] * (width // LANES), axis=1)


def wait_bytes(ref, sem):
    pltpu.make_async_copy(ref, ref, sem).wait()


def make_codebook(i, bas, cmap, cb, sq):
    part = slice(i * CHUNK, (i + 1) * CHUNK)
    code = dot(bas[part, :], cmap[...]).astype(BF16)
    cb[part, :] = code
    wide_code = code.astype(F32)
    square = wide_code * wide_code
    upper = square.astype(BF16)
    lower = (square - upper.astype(F32)).astype(BF16)
    ones = jnp.full((16, 2 * LANES), -0.0625, BF16)
    total = dot(ones, jnp.concatenate([upper, lower], axis=1), NT)
    sq[:, part] = total[:8]


def group_scores(x_group, cb, sq, s_buf, top):
    codes = cb.shape[0]
    s = dot(x_group[...], cb[...], NT) + sq[0:1, :]
    s_buf[...] = s
    best = s[:, :LANES]
    for j in range(1, codes // LANES):
        best = jnp.maximum(best, s[:, j * LANES:(j + 1) * LANES])
    top[...] = jnp.broadcast_to(jnp.max(best, axis=1, keepdims=True), best.shape)


def group_weights(slots, s_buf, top, bas, w_buf, acc):
    codes = bas.shape[0]
    w = jnp.exp(s_buf[...] - wide(top[...], codes)).astype(BF16)
    rows = w.shape[0] // len(slots)
    for j, slot in enumerate(slots):
        w_buf[slot * rows:(slot + 1) * rows, :] = w[j * rows:(j + 1) * rows]
    acc[...] = dot(w, jnp.concatenate([bas[...], jnp.ones((codes, LANES), BF16)], axis=1))


def lanes_of(columns):
    rows = columns.shape[0]
    eye = lax.broadcasted_iota(jnp.int32, (LANES, LANES), 0) == lax.broadcasted_iota(
        jnp.int32, (LANES, LANES), 1
    )
    out = []
    for g in range(rows // LANES):
        part = jnp.where(eye, columns[g * LANES:(g + 1) * LANES], 0.0)
        out.append(jnp.sum(part, axis=0, keepdims=True))
    return jnp.concatenate(out, axis=0)


def usage_half(r3, w_buf, start, out):
    width = w_buf.shape[1] // 2
    u = jnp.sum(dot(r3, w_buf[:, pl.ds(start, width)]), axis=0, keepdims=True)
    for j in range(width // LANES):
        out[j:j + 1, :] = u[:, j * LANES:(j + 1) * LANES]


def kernel(n_dp, n_code, x_ref, basis_ref, map_ref, q_ref, u_ref, g_ref,
           bas, cmap, cb, sq, x_all, x_group, s_buf, top, w_buf, acc, m_col, t_col,
           lse, w_send, w_recv, fac, w_all,
           u_row, u_send, u_level, u_all,
           load_sem, send_sem, recv_sem):
    dp = lax.axis_index("dp")
    code = lax.axis_index("code")
    z_lo, y = code // RING, lax.rem(code, RING)
    core = lax.rem(dp, 2)
    x_pos = lax.rem(dp // 2, X)
    z_hi = dp // (2 * X)
    codes = basis_ref.shape[0]
    nblk = codes // CHUNK
    rows = x_ref.shape[0]
    tokens = rows * n_code
    groups = tokens // LANES

    def peer_code(offset):
        return lax.rem(z_lo + offset[0], n_code // RING) * RING + lax.rem(y + offset[1], RING)

    owners = [[peer_code(o) for o in group] for group in NEAR]
    far_first = owners[2] + owners[1][::-1] + owners[0][:0:-1]
    rank = lax.rem(dp, 2 * X)

    def peer_dp(a, b, c):
        return (lax.rem(z_hi + a, ZH) * X + lax.rem(x_pos + b, X)) * 2 + c

    level_other = [peer_dp(0, b, 1 - core) for b in (2, 1, 3, 0)]
    level_same = [peer_dp(0, b, core) for b in (2, 1, 3)]
    column = [peer_dp(a, 0, c) for a in (2, 1, 3) for c in (core, 1 - core)]

    barrier = pltpu.get_barrier_semaphore()
    for p in far_first:
        pl.semaphore_signal(barrier, inc=1, device_id=(dp, p), device_id_type=MESH)
    for d in column + level_other + level_same:
        pl.semaphore_signal(barrier, inc=1, device_id=(d, code), device_id_type=MESH)

    x_load = pltpu.make_async_copy(x_ref, x_all.at[code], load_sem.at[nblk])
    m_load = pltpu.make_async_copy(map_ref, cmap, load_sem.at[nblk + 1])
    b_loads = [
        pltpu.make_async_copy(
            basis_ref.at[pl.ds(i * CHUNK, CHUNK)], bas.at[pl.ds(i * CHUNK, CHUNK)], load_sem.at[i]
        )
        for i in range(nblk)
    ]
    x_load.start()
    m_load.start()
    for load in b_loads:
        load.start()

    def remote(src, dst, phase, device):
        return pltpu.make_async_remote_copy(
            src_ref=src, dst_ref=dst, send_sem=send_sem.at[phase], recv_sem=recv_sem.at[phase],
            device_id=device, device_id_type=MESH,
        )

    x_load.wait()
    pl.semaphore_wait(barrier, n_code - 1 + len(column + level_other + level_same))

    def send_sums(g):
        for p, offset in zip(owners[g], NEAR[g]):
            if offset != (0, 0):
                remote(w_send.at[p], w_recv.at[code], 4, (dp, p)).start()

    for g in range(len(NEAR)):
        for p, offset in zip(owners[g], NEAR[g]):
            if offset != (0, 0):
                remote(x_all.at[code], x_all.at[code], g, (dp, p)).start()

    m_load.wait()
    for i in range(nblk):
        b_loads[i].wait()
        make_codebook(i, bas, cmap, cb, sq)

    always = lax.rem(dp * (dp + 1), 2) == 0
    for g, group in enumerate(owners):
        size = len(group) * rows
        arriving = len(group) - (1 if g == 0 else 0)
        wait_bytes(x_all.at[pl.ds(0, arriving)], recv_sem.at[g])
        for j, o in enumerate(group):
            x_group[j * rows:(j + 1) * rows, :] = x_all[o] * jnp.asarray(0.125, BF16)
        some = pl.ds(0, size)
        slots = [o[0] * RING + o[1] for o in NEAR[g]]
        group_scores(x_group.at[some], cb, sq, s_buf.at[some], top.at[some])
        pl.when(always)(lambda: group_weights(slots, s_buf.at[some], top.at[some], bas, w_buf, acc.at[some]))
        for j, o in enumerate(group):
            part = slice(j * rows, (j + 1) * rows)
            place = pl.ds(pl.multiple_of(o * rows, rows), rows)
            m_col[place, :] = top[part, :]
            t_col[place, :] = acc[part, LANES:]
            w_send[o] = acc[part, :LANES].astype(BF16)
        if g < 2:
            send_sums(g)

    lse[code] = jnp.concatenate([lanes_of(m_col[...]), lanes_of(t_col[...])], axis=0)
    for p in far_first:
        remote(lse.at[code], lse.at[code], 3, (dp, p)).start()
    send_sums(2)
    w_recv[code] = w_send[code]

    others = pl.ds(0, n_code - 1)
    wait_bytes(lse.at[others], recv_sem.at[3])
    tops = lse[:, :groups, :]
    best = jnp.max(tops, axis=0)
    factor = jnp.exp(tops - best[None])
    total = jnp.sum(factor * lse[:, groups:, :], axis=0)
    own = jnp.exp(lse[code, :groups, :] - best) / total
    width = RING * rows
    place = lax.broadcasted_iota(jnp.int32, (16, width), 0)
    halves = []
    for h in range(tokens // width):
        each = width // LANES
        row = jnp.concatenate([own[h * each + g:h * each + g + 1] for g in range(each)], axis=1)
        pieces = jnp.zeros((16, width), F32)
        for j, piece in enumerate(split_three(row)):
            pieces = jnp.where(place == j, jnp.broadcast_to(piece.astype(F32), pieces.shape), pieces)
        halves.append(pieces)
    if len(halves) == 2:
        halves = [jnp.where(z_lo == 0, halves[0], halves[1]), jnp.where(z_lo == 0, halves[1], halves[0])]
    turn = lax.rem((RING - y) * rows, width)
    r3 = jnp.concatenate([pltpu.roll(h, turn, 1) for h in halves], axis=1).astype(BF16)

    half = codes // 2
    for k in (0, 1):
        pl.when(core == 1 - k)(lambda k=k: usage_half(r3, w_buf, k * half, u_row))
    u_send[0] = u_row[...].astype(BF16)
    for d in level_other:
        remote(u_send.at[0], u_level.at[rank], 5, (d, code)).start()
    for k in (0, 1):
        pl.when(core == k)(lambda k=k: usage_half(r3, w_buf, k * half, u_row))
    u_send[1] = u_row[...].astype(BF16)
    for d in level_same:
        remote(u_send.at[1], u_level.at[rank], 5, (d, code)).start()
    u_level[rank] = u_send[1]

    scaled = factor / total[None]
    for g in range(groups):
        fac[g, :n_code] = scaled[:, g, :]
        fac[g, n_code:] = jnp.zeros((LANES - n_code, LANES), F32)
    per = LANES // rows
    fac[0] = jnp.transpose(fac[code // per])
    mine = fac[0, pl.ds(pl.multiple_of(lax.rem(code, per) * rows, rows), rows), :]

    wait_bytes(w_recv.at[others], recv_sem.at[4])
    w_own = jnp.zeros((rows, LANES), F32)
    for c in range(n_code):
        w_own = w_own + mine[:, c:c + 1] * w_recv[c].astype(F32)
    w_all[code] = w_own.astype(BF16)
    for p in far_first:
        remote(w_all.at[code], w_all.at[code], 7, (dp, p)).start()

    soft_own = jnp.zeros((rows, LANES), F32)
    for piece in split_three(w_own):
        soft_own = soft_own + dot(piece, cmap[...])
    q_ref[...] = soft_own.astype(BF16)

    level = pl.ds(0, len(level_other + level_same))
    wait_bytes(u_level.at[level], recv_sem.at[5])
    u_all[z_hi, core] = jnp.sum(u_level[...].astype(F32), axis=0).astype(BF16)
    last = peer_dp(0, 0, 1 - core)
    for d in column + [last]:
        remote(u_all.at[z_hi, core], u_all.at[z_hi, core], 6, (d, code)).start()

    wait_bytes(w_all.at[others], recv_sem.at[7])
    w_tile = w_all[...].reshape(tokens, LANES)
    x_tile = x_all[...].reshape(tokens, LANES)
    errors = (dot(w_tile, cmap[...]) - x_tile.astype(F32)).astype(BF16)
    g_ref[...] = dot(w_tile, errors, TN) * (1.0 / math.sqrt(tokens))

    wait_bytes(u_level.at[level], recv_sem.at[6])
    scale = (codes * n_code) / (tokens * n_dp)
    u_ref[...] = jnp.sum(u_all[...].astype(F32), axis=0) * scale

    wait_bytes(x_all.at[pl.ds(0, len(NEAR[0]) - 1)], send_sem.at[0])
    wait_bytes(x_all.at[pl.ds(0, len(NEAR[1]))], send_sem.at[1])
    wait_bytes(x_all.at[pl.ds(0, len(NEAR[2]))], send_sem.at[2])
    wait_bytes(lse.at[others], send_sem.at[3])
    wait_bytes(w_send.at[others], send_sem.at[4])
    wait_bytes(u_level.at[level], send_sem.at[5])
    wait_bytes(u_level.at[level], send_sem.at[6])
    wait_bytes(w_all.at[others], send_sem.at[7])


def deliver(q_in, u_in, g_in, q_ref, u_ref, g_ref, sem):
    copies = [
        pltpu.make_async_copy(src, dst, sem.at[i])
        for i, (src, dst) in enumerate(((g_in, g_ref), (u_in, u_ref), (q_in, q_ref)))
    ]
    for copy in copies:
        copy.start()
    for copy in copies:
        copy.wait()


def body(n_dp, n_code, latents, basis, code_map):
    rows, width = latents.shape
    codes = basis.shape[0]
    nblk = codes // CHUNK
    tokens = rows * n_code
    half = codes // 2
    vm = pltpu.VMEM
    anywhere = pl.BlockSpec(memory_space=pl.ANY)
    quantized, usage, grad = pl.pallas_call(
        functools.partial(kernel, n_dp, n_code),
        out_shape=(
            vm((rows, width), BF16),
            vm((2, half // LANES, LANES), F32),
            vm((width, width), F32),
        ),
        in_specs=[pl.BlockSpec(memory_space=pltpu.HBM)] * 3,
        out_specs=[pl.BlockSpec(memory_space=vm)] * 3,
        scratch_shapes=[
            vm((codes, width), BF16),
            vm((width, width), BF16),
            vm((codes, width), BF16),
            vm((8, codes), F32),
            vm((n_code, rows, width), BF16),
            vm((tokens // 2, width), BF16),
            vm((tokens // 2, codes), F32),
            vm((tokens // 2, LANES), F32),
            vm((tokens, codes), BF16),
            vm((tokens // 2, 2 * width), F32),
            vm((tokens, LANES), F32),
            vm((tokens, LANES), F32),
            vm((n_code, 2 * tokens // LANES, LANES), F32),
            vm((n_code, rows, width), BF16),
            vm((n_code, rows, width), BF16),
            vm((tokens // LANES, LANES, LANES), F32),
            vm((n_code, rows, width), BF16),
            vm((half // LANES, LANES), F32),
            vm((2, half // LANES, LANES), BF16),
            vm((2 * X, half // LANES, LANES), BF16),
            vm((ZH, 2, half // LANES, LANES), BF16),
            pltpu.SemaphoreType.DMA((nblk + 2,)),
            pltpu.SemaphoreType.DMA((8,)),
            pltpu.SemaphoreType.DMA((8,)),
        ],
        compiler_params=pltpu.CompilerParams(
            collective_id=0, has_side_effects=True, vmem_limit_bytes=40 * 1024 * 1024
        ),
    )(*(pltpu.with_memory_space_constraint(a, pltpu.HBM) for a in (latents, basis, code_map)))
    return pl.pallas_call(
        deliver,
        out_shape=(
            jax.ShapeDtypeStruct((rows, width), BF16),
            jax.ShapeDtypeStruct((codes,), F32),
            jax.ShapeDtypeStruct((width, width), F32),
        ),
        in_specs=[anywhere] * 3,
        out_specs=[anywhere] * 3,
        scratch_shapes=[pltpu.SemaphoreType.DMA((3,))],
    )(*(pltpu.with_memory_space_constraint(a, vm) for a in (quantized, usage.reshape(codes), grad)))


def solution(mesh):
    return jax.shard_map(
        functools.partial(body, mesh.shape["dp"], mesh.shape["code"]),
        mesh=mesh,
        in_specs=(P(("dp", "code"), None), P("code", None), P()),
        out_specs=(P(("dp", "code"), None), P("code"), P("dp", None)),
        check_vma=False,
    )
```

```python
import functools
import math

import jax
import jax.numpy as jnp
from jax import lax
from jax.experimental import pallas as pl
from jax.experimental.pallas import tpu as pltpu
from jax.sharding import PartitionSpec as P

MESH = pl.DeviceIdType.MESH
F32 = jnp.float32
BF16 = jnp.bfloat16
NN = (((1,), (0,)), ((), ()))
NT = (((1,), (1,)), ((), ()))
TN = (((0,), (0,)), ((), ()))
LANES = 128
CHUNK = 2048

RING = 8
NEAR = (
    ((0, 0), (0, 1), (0, 7), (1, 0)),
    ((0, 2), (0, 6), (1, 1), (1, 7)),
    ((1, 4), (0, 4), (1, 3), (1, 5), (0, 3), (0, 5), (1, 2), (1, 6)),
)
X = 4
ZH = 4


def dot(a, b, dims=NN):
    return lax.dot_general(a, b, dims, preferred_element_type=F32)


def split_three(values):
    upper = values.astype(BF16)
    rest = values - upper.astype(F32)
    middle = rest.astype(BF16)
    lower = (rest - middle.astype(F32)).astype(BF16)
    return (upper, middle, lower)


def wide(column, width):
    return jnp.concatenate([column] * (width // LANES), axis=1)


def wait_bytes(ref, sem):
    pltpu.make_async_copy(ref, ref, sem).wait()


def make_codebook(i, bas, cmap, cb, sq):
    part = slice(i * CHUNK, (i + 1) * CHUNK)
    code = dot(bas[part, :], cmap[...]).astype(BF16)
    cb[part, :] = code
    wide_code = code.astype(F32)
    square = wide_code * wide_code
    upper = square.astype(BF16)
    lower = (square - upper.astype(F32)).astype(BF16)
    ones = jnp.full((16, 2 * LANES), -0.0625, BF16)
    total = dot(ones, jnp.concatenate([upper, lower], axis=1), NT)
    sq[:, part] = total[:8]


def group_scores(x_group, cb, sq, s_buf, top):
    codes = cb.shape[0]
    s = dot(x_group[...], cb[...], NT) + sq[0:1, :]
    s_buf[...] = s
    best = s[:, :LANES]
    for j in range(1, codes // LANES):
        best = jnp.maximum(best, s[:, j * LANES:(j + 1) * LANES])
    top[...] = jnp.broadcast_to(jnp.max(best, axis=1, keepdims=True), best.shape)


def group_weights(slots, s_buf, top, bas, w_buf, acc):
    codes = bas.shape[0]
    w = jnp.exp(s_buf[...] - wide(top[...], codes)).astype(BF16)
    rows = w.shape[0] // len(slots)
    for j, slot in enumerate(slots):
        w_buf[slot * rows:(slot + 1) * rows, :] = w[j * rows:(j + 1) * rows]
    acc[...] = dot(w, jnp.concatenate([bas[...], jnp.ones((codes, LANES), BF16)], axis=1))


def lanes_of(columns):
    rows = columns.shape[0]
    eye = lax.broadcasted_iota(jnp.int32, (LANES, LANES), 0) == lax.broadcasted_iota(
        jnp.int32, (LANES, LANES), 1
    )
    out = []
    for g in range(rows // LANES):
        part = jnp.where(eye, columns[g * LANES:(g + 1) * LANES], 0.0)
        out.append(jnp.sum(part, axis=0, keepdims=True))
    return jnp.concatenate(out, axis=0)


def usage_half(r3, w_buf, start, out):
    width = w_buf.shape[1] // 2
    u = jnp.sum(dot(r3, w_buf[:, pl.ds(start, width)]), axis=0, keepdims=True)
    for j in range(width // LANES):
        out[j:j + 1, :] = u[:, j * LANES:(j + 1) * LANES]


def kernel(n_dp, n_code, x_ref, basis_ref, map_ref, q_ref, u_ref, g_ref,
           bas, cmap, cb, sq, x_all, x_group, s_buf, top, w_buf, acc, m_col, t_col,
           lse, w_send, w_recv, fac, w_all,
           u_row, u_send, u_level, u_all,
           load_sem, send_sem, recv_sem):
    dp = lax.axis_index("dp")
    code = lax.axis_index("code")
    z_lo, y = code // RING, lax.rem(code, RING)
    core = lax.rem(dp, 2)
    x_pos = lax.rem(dp // 2, X)
    z_hi = dp // (2 * X)
    codes = basis_ref.shape[0]
    nblk = codes // CHUNK
    rows = x_ref.shape[0]
    tokens = rows * n_code
    groups = tokens // LANES

    def peer_code(offset):
        return lax.rem(z_lo + offset[0], n_code // RING) * RING + lax.rem(y + offset[1], RING)

    owners = [[peer_code(o) for o in group] for group in NEAR]
    far_first = owners[2] + owners[1][::-1] + owners[0][:0:-1]
    rank = lax.rem(dp, 2 * X)

    def peer_dp(a, b, c):
        return (lax.rem(z_hi + a, ZH) * X + lax.rem(x_pos + b, X)) * 2 + c

    level_other = [peer_dp(0, b, 1 - core) for b in (2, 1, 3, 0)]
    level_same = [peer_dp(0, b, core) for b in (2, 1, 3)]
    column = [peer_dp(a, 0, c) for a in (2, 1, 3) for c in (core, 1 - core)]

    barrier = pltpu.get_barrier_semaphore()
    for p in far_first:
        pl.semaphore_signal(barrier, inc=1, device_id=(dp, p), device_id_type=MESH)
    for d in column + level_other + level_same:
        pl.semaphore_signal(barrier, inc=1, device_id=(d, code), device_id_type=MESH)

    x_load = pltpu.make_async_copy(x_ref, x_all.at[code], load_sem.at[nblk])
    m_load = pltpu.make_async_copy(map_ref, cmap, load_sem.at[nblk + 1])
    b_loads = [
        pltpu.make_async_copy(
            basis_ref.at[pl.ds(i * CHUNK, CHUNK)], bas.at[pl.ds(i * CHUNK, CHUNK)], load_sem.at[i]
        )
        for i in range(nblk)
    ]
    x_load.start()
    m_load.start()
    for load in b_loads:
        load.start()

    def remote(src, dst, phase, device):
        return pltpu.make_async_remote_copy(
            src_ref=src, dst_ref=dst, send_sem=send_sem.at[phase], recv_sem=recv_sem.at[phase],
            device_id=device, device_id_type=MESH,
        )

    x_load.wait()
    pl.semaphore_wait(barrier, n_code - 1 + len(column + level_other + level_same))

    def send_sums(g):
        for p, offset in zip(owners[g], NEAR[g]):
            if offset != (0, 0):
                remote(w_send.at[p], w_recv.at[code], 4, (dp, p)).start()

    for g in range(len(NEAR)):
        for p, offset in zip(owners[g], NEAR[g]):
            if offset != (0, 0):
                remote(x_all.at[code], x_all.at[code], g, (dp, p)).start()

    m_load.wait()
    for i in range(nblk):
        b_loads[i].wait()
        make_codebook(i, bas, cmap, cb, sq)

    always = lax.rem(dp * (dp + 1), 2) == 0
    for g, group in enumerate(owners):
        size = len(group) * rows
        arriving = len(group) - (1 if g == 0 else 0)
        wait_bytes(x_all.at[pl.ds(0, arriving)], recv_sem.at[g])
        for j, o in enumerate(group):
            x_group[j * rows:(j + 1) * rows, :] = x_all[o] * jnp.asarray(0.125, BF16)
        some = pl.ds(0, size)
        slots = [o[0] * RING + o[1] for o in NEAR[g]]
        group_scores(x_group.at[some], cb, sq, s_buf.at[some], top.at[some])
        pl.when(always)(lambda: group_weights(slots, s_buf.at[some], top.at[some], bas, w_buf, acc.at[some]))
        for j, o in enumerate(group):
            part = slice(j * rows, (j + 1) * rows)
            place = pl.ds(pl.multiple_of(o * rows, rows), rows)
            m_col[place, :] = top[part, :]
            t_col[place, :] = acc[part, LANES:]
            w_send[o] = acc[part, :LANES].astype(BF16)
        if g < 2:
            send_sums(g)

    lse[code] = jnp.concatenate([lanes_of(m_col[...]), lanes_of(t_col[...])], axis=0)
    for g in (2, 1, 0):
        for p, offset in zip(owners[g], NEAR[g]):
            if offset != (0, 0):
                remote(lse.at[code], lse.at[code], 3 if g == 2 else 8, (dp, p)).start()
    w_recv[code] = w_send[code]
    others = pl.ds(0, n_code - 1)
    wait_bytes(lse.at[pl.ds(0, 7)], recv_sem.at[8])
    send_sums(2)
    wait_bytes(lse.at[pl.ds(0, 8)], recv_sem.at[3])
    tops = lse[:, :groups, :]
    best = jnp.max(tops, axis=0)
    factor = jnp.exp(tops - best[None])
    total = jnp.sum(factor * lse[:, groups:, :], axis=0)
    own = jnp.exp(lse[code, :groups, :] - best) / total
    width = RING * rows
    place = lax.broadcasted_iota(jnp.int32, (16, width), 0)
    halves = []
    for h in range(tokens // width):
        each = width // LANES
        row = jnp.concatenate([own[h * each + g:h * each + g + 1] for g in range(each)], axis=1)
        pieces = jnp.zeros((16, width), F32)
        for j, piece in enumerate(split_three(row)):
            pieces = jnp.where(place == j, jnp.broadcast_to(piece.astype(F32), pieces.shape), pieces)
        halves.append(pieces)
    if len(halves) == 2:
        halves = [jnp.where(z_lo == 0, halves[0], halves[1]), jnp.where(z_lo == 0, halves[1], halves[0])]
    turn = lax.rem((RING - y) * rows, width)
    r3 = jnp.concatenate([pltpu.roll(h, turn, 1) for h in halves], axis=1).astype(BF16)

    half = codes // 2
    for k in (0, 1):
        pl.when(core == 1 - k)(lambda k=k: usage_half(r3, w_buf, k * half, u_row))
    u_send[0] = u_row[...].astype(BF16)
    for d in level_other:
        remote(u_send.at[0], u_level.at[rank], 5, (d, code)).start()
    for k in (0, 1):
        pl.when(core == k)(lambda k=k: usage_half(r3, w_buf, k * half, u_row))
    u_send[1] = u_row[...].astype(BF16)
    for d in level_same:
        remote(u_send.at[1], u_level.at[rank], 5, (d, code)).start()
    u_level[rank] = u_send[1]

    scaled = factor / total[None]
    for g in range(groups):
        fac[g, :n_code] = scaled[:, g, :]
        fac[g, n_code:] = jnp.zeros((LANES - n_code, LANES), F32)
    per = LANES // rows
    fac[0] = jnp.transpose(fac[code // per])
    mine = fac[0, pl.ds(pl.multiple_of(lax.rem(code, per) * rows, rows), rows), :]

    wait_bytes(w_recv.at[others], recv_sem.at[4])
    w_own = jnp.zeros((rows, LANES), F32)
    for c in range(n_code):
        w_own = w_own + mine[:, c:c + 1] * w_recv[c].astype(F32)
    w_all[code] = w_own.astype(BF16)
    for p in far_first:
        remote(w_all.at[code], w_all.at[code], 7, (dp, p)).start()

    soft_own = jnp.zeros((rows, LANES), F32)
    for piece in split_three(w_own):
        soft_own = soft_own + dot(piece, cmap[...])
    q_ref[...] = soft_own.astype(BF16)

    level = pl.ds(0, len(level_other + level_same))
    wait_bytes(u_level.at[level], recv_sem.at[5])
    u_all[z_hi, core] = jnp.sum(u_level[...].astype(F32), axis=0).astype(BF16)
    last = peer_dp(0, 0, 1 - core)
    for d in column + [last]:
        remote(u_all.at[z_hi, core], u_all.at[z_hi, core], 6, (d, code)).start()

    wait_bytes(w_all.at[others], recv_sem.at[7])
    w_tile = w_all[...].reshape(tokens, LANES)
    x_tile = x_all[...].reshape(tokens, LANES)
    errors = (dot(w_tile, cmap[...]) - x_tile.astype(F32)).astype(BF16)
    g_ref[...] = dot(w_tile, errors, TN) * (1.0 / math.sqrt(tokens))

    wait_bytes(u_level.at[level], recv_sem.at[6])
    scale = (codes * n_code) / (tokens * n_dp)
    u_ref[...] = jnp.sum(u_all[...].astype(F32), axis=0) * scale

    wait_bytes(x_all.at[pl.ds(0, len(NEAR[0]) - 1)], send_sem.at[0])
    wait_bytes(x_all.at[pl.ds(0, len(NEAR[1]))], send_sem.at[1])
    wait_bytes(x_all.at[pl.ds(0, len(NEAR[2]))], send_sem.at[2])
    wait_bytes(lse.at[pl.ds(0, 8)], send_sem.at[3])
    wait_bytes(lse.at[pl.ds(0, 7)], send_sem.at[8])
    wait_bytes(w_send.at[others], send_sem.at[4])
    wait_bytes(u_level.at[level], send_sem.at[5])
    wait_bytes(u_level.at[level], send_sem.at[6])
    wait_bytes(w_all.at[others], send_sem.at[7])


def deliver(q_in, u_in, g_in, q_ref, u_ref, g_ref, sem):
    copies = [
        pltpu.make_async_copy(src, dst, sem.at[i])
        for i, (src, dst) in enumerate(((g_in, g_ref), (u_in, u_ref), (q_in, q_ref)))
    ]
    for copy in copies:
        copy.start()
    for copy in copies:
        copy.wait()


def body(n_dp, n_code, latents, basis, code_map):
    rows, width = latents.shape
    codes = basis.shape[0]
    nblk = codes // CHUNK
    tokens = rows * n_code
    half = codes // 2
    vm = pltpu.VMEM
    anywhere = pl.BlockSpec(memory_space=pl.ANY)
    quantized, usage, grad = pl.pallas_call(
        functools.partial(kernel, n_dp, n_code),
        out_shape=(
            vm((rows, width), BF16),
            vm((2, half // LANES, LANES), F32),
            vm((width, width), F32),
        ),
        in_specs=[pl.BlockSpec(memory_space=pltpu.HBM)] * 3,
        out_specs=[pl.BlockSpec(memory_space=vm)] * 3,
        scratch_shapes=[
            vm((codes, width), BF16),
            vm((width, width), BF16),
            vm((codes, width), BF16),
            vm((8, codes), F32),
            vm((n_code, rows, width), BF16),
            vm((tokens // 2, width), BF16),
            vm((tokens // 2, codes), F32),
            vm((tokens // 2, LANES), F32),
            vm((tokens, codes), BF16),
            vm((tokens // 2, 2 * width), F32),
            vm((tokens, LANES), F32),
            vm((tokens, LANES), F32),
            vm((n_code, 2 * tokens // LANES, LANES), F32),
            vm((n_code, rows, width), BF16),
            vm((n_code, rows, width), BF16),
            vm((tokens // LANES, LANES, LANES), F32),
            vm((n_code, rows, width), BF16),
            vm((half // LANES, LANES), F32),
            vm((2, half // LANES, LANES), BF16),
            vm((2 * X, half // LANES, LANES), BF16),
            vm((ZH, 2, half // LANES, LANES), BF16),
            pltpu.SemaphoreType.DMA((nblk + 2,)),
            pltpu.SemaphoreType.DMA((9,)),
            pltpu.SemaphoreType.DMA((9,)),
        ],
        compiler_params=pltpu.CompilerParams(
            collective_id=0, has_side_effects=True, vmem_limit_bytes=40 * 1024 * 1024
        ),
    )(*(pltpu.with_memory_space_constraint(a, pltpu.HBM) for a in (latents, basis, code_map)))
    return pl.pallas_call(
        deliver,
        out_shape=(
            jax.ShapeDtypeStruct((rows, width), BF16),
            jax.ShapeDtypeStruct((codes,), F32),
            jax.ShapeDtypeStruct((width, width), F32),
        ),
        in_specs=[anywhere] * 3,
        out_specs=[anywhere] * 3,
        scratch_shapes=[pltpu.SemaphoreType.DMA((3,))],
    )(*(pltpu.with_memory_space_constraint(a, vm) for a in (quantized, usage.reshape(codes), grad)))


def solution(mesh):
    return jax.shard_map(
        functools.partial(body, mesh.shape["dp"], mesh.shape["code"]),
        mesh=mesh,
        in_specs=(P(("dp", "code"), None), P("code", None), P()),
        out_specs=(P(("dp", "code"), None), P("code"), P("dp", None)),
        check_vma=False,
    )
```
